256 devices in a mesh: row: 8 (over y, core), col: 32 (over x, z).
Axes of the slice: x: 4, y: 4, z: 8, core: 2. Of those that a mesh axis runs over, the one named last changes fastest.
Arguments:
- gradient: bfloat16 [3584, 12288], P('row', 'col'), may hold values from -54 to 54
- momentum: float32 [3584, 12288], P('row', 'col'), may hold values from -54 to 54
Outputs:
- update_matrix: bfloat16 [3584, 12288], P('row', 'col')
- new_momentum: float32 [3584, 12288], P('row', 'col')
The draws below stay inside these ranges and needn't reach their ends.
All inputs are finite; a program needn't handle non-finite values.
Results may differ from the reference program's by a relative error of at most 0.013.
Values may be sent and summed in bfloat16 or wider, within the bound.
No kernel may reach another device: no remote copies, remote signals or barrier semaphores. Data moves between devices by JAX's collectives and lax.ppermute only.
A program may use at most 64 MiB of HBM per device.

```python
import math
import jax
import jax.numpy as jnp

M = 3584
N = 12288
ITERS = 2


def ramped_rows(key):
    first, second = jax.random.split(key)
    position = jnp.arange(M).astype(jnp.float32) / M
    trend = jnp.exp(position * math.log(3.0))[:, None]
    factor = jnp.exp(jax.random.uniform(first, (M, 1), jnp.float32) * math.log(3.0))
    noise = jnp.clip(jax.random.normal(second, (M, N), jnp.float32), -4.0, 4.0)
    values = noise + 0.5 * jnp.roll(noise, M // 2, axis=0)
    return values * trend * factor


def draw_gradient(key, part):
    return ramped_rows(jax.random.fold_in(key, 11)).astype(jnp.bfloat16)


def draw_momentum(key, part):
    return ramped_rows(jax.random.fold_in(key, 23)).astype(jnp.float32)


def setup_inputs(seed: int = 0) -> dict:
    key_of = jax.random.split(jax.random.key(seed), 3)
    gradient = draw_gradient(jax.random.fold_in(key_of[2], 71), 0)
    momentum = draw_momentum(jax.random.fold_in(key_of[2], 71), 0)
    return {"gradient": gradient, "momentum": momentum}


MOMENTUM_DECAY = 0.95
EPSILON = 1e-07
COEF_LINEAR = 3.4445
COEF_CUBIC = -4.775
COEF_QUINTIC = 2.0315

def reference(gradient, momentum):
    grad32 = gradient.astype(jnp.float32)
    buffer = MOMENTUM_DECAY * momentum + grad32
    nesterov = grad32 + MOMENTUM_DECAY * buffer
    base = nesterov.astype(jnp.bfloat16)
    raw = jnp.dot(base, base.T, preferred_element_type=jnp.float32)
    quartic = jnp.sum(raw * raw)
    scale = 1.0 / jnp.sqrt(jnp.sqrt(quartic) + EPSILON)
    iterate = (base.astype(jnp.float32) * scale).astype(jnp.bfloat16)
    combined = iterate.astype(jnp.float32)
    for iteration in range(ITERS):
        if iteration == 0:
            gram = (raw * (scale * scale)).astype(jnp.bfloat16)
        else:
            gram = jnp.dot(iterate, iterate.T, preferred_element_type=jnp.float32).astype(jnp.bfloat16)
        product = jnp.dot(gram, iterate, preferred_element_type=jnp.float32)
        second = jnp.dot(gram, product.astype(jnp.bfloat16), preferred_element_type=jnp.float32)
        combined = COEF_LINEAR * iterate.astype(jnp.float32) + COEF_CUBIC * product + COEF_QUINTIC * second
        if iteration + 1 < ITERS:
            iterate = combined.astype(jnp.bfloat16)
    update_matrix = (combined * (0.2 * math.sqrt(max(M, N)))).astype(jnp.bfloat16)
    return (update_matrix, buffer)
```

```python
import functools
import math

import jax
import jax.numpy as jnp
from jax import lax
from jax.experimental import pallas as pl
from jax.experimental.pallas import tpu as pltpu
from jax.sharding import PartitionSpec as P

M = 3584
N = 12288
ROWS = 8
COLS = 32
X_CHIPS = 4
Z_CHIPS = 8

MOMENTUM_DECAY = 0.95
EPSILON = 1e-07
COEF_LINEAR = 3.4445
COEF_CUBIC = -4.775
COEF_QUINTIC = 2.0315
UPDATE_SCALE = 0.2 * math.sqrt(max(M, N))

BLOCK = 512
BLOCKS = M // BLOCK
KEPT = (BLOCKS + 1) // 2
HALF = BLOCK // 2
UNITS = BLOCKS * KEPT * 2 // ROWS
PANEL_COLS = N // COLS
OWN_COLS = PANEL_COLS // ROWS
OWN_ROWS = M // ROWS

X_GROUPS = [[x * Z_CHIPS + z for x in range(X_CHIPS)] for z in range(Z_CHIPS)]
Z_GROUPS = [[x * Z_CHIPS + z for z in range(Z_CHIPS)] for x in range(X_CHIPS)]


def dot_nt(left, right):
    return lax.dot_general(
        left, right, (((1,), (1,)), ((), ())), preferred_element_type=jnp.float32
    )


def gram_kernel(panel_ref, units_ref, columns_ref):
    row = lax.axis_index("row")
    unit = pl.program_id(0)
    number = row * UNITS + unit
    block, half = number // 2, number % 2
    i, d = block // KEPT, block % KEPT
    j = lax.rem(i + d, BLOCKS)
    left = panel_ref[pl.ds(pl.multiple_of(i * BLOCK + half * HALF, HALF), HALF), :]
    right = panel_ref[pl.ds(pl.multiple_of(j * BLOCK, BLOCK), BLOCK), :]
    units_ref[...] = dot_nt(left, right).astype(units_ref.dtype)
    wanted = row * OWN_COLS + lax.broadcasted_iota(jnp.int32, (OWN_COLS, PANEL_COLS), 0)
    column = lax.broadcasted_iota(jnp.int32, (OWN_COLS, PANEL_COLS), 1)
    pick = jnp.where(wanted == column, 1.0, 0.0).astype(jnp.bfloat16)
    rows = panel_ref[pl.ds(pl.multiple_of(unit * BLOCK, BLOCK), BLOCK), :]
    columns_ref[...] = dot_nt(pick, rows).astype(columns_ref.dtype)


def partial_gram(panel):
    return pl.pallas_call(
        gram_kernel,
        grid=(UNITS,),
        out_shape=(
            jax.ShapeDtypeStruct((UNITS * HALF, BLOCK), jnp.bfloat16),
            jax.ShapeDtypeStruct((OWN_COLS, M), jnp.bfloat16),
        ),
        in_specs=[pl.BlockSpec((M, PANEL_COLS), lambda u: (0, 0))],
        out_specs=(
            pl.BlockSpec((HALF, BLOCK), lambda u: (u, 0)),
            pl.BlockSpec((OWN_COLS, BLOCK), lambda u: (0, u)),
        ),
        compiler_params=pltpu.CompilerParams(vmem_limit_bytes=32 * 2**20),
        name="partial_gram",
    )(panel)


def times_gram(gram_ref, value_ref, write):
    for j in range(BLOCKS):
        total = None
        for d in range(KEPT):
            i = (j - d) % BLOCKS
            term = jnp.dot(
                value_ref[:, i * BLOCK : (i + 1) * BLOCK],
                gram_ref[i * KEPT + d],
                preferred_element_type=jnp.float32,
            )
            total = term if total is None else total + term
        for d in range(1, KEPT):
            i = (j + d) % BLOCKS
            total = total + dot_nt(
                value_ref[:, i * BLOCK : (i + 1) * BLOCK], gram_ref[j * KEPT + d]
            )
        write(j, total)


def newton_schulz_kernel(gram_ref, base_ref, out_ref, value, point, product):
    def square_sum(block):
        rows = jnp.zeros((8, BLOCK), jnp.float32)
        for r in range(0, BLOCK, 64):
            part = gram_ref[block, r : r + 64, :].astype(jnp.float32)
            rows = rows + jnp.sum((part * part).reshape(8, 8, BLOCK), axis=0)
        return rows

    def squares(i, total):
        own = square_sum(i * KEPT)
        others = square_sum(i * KEPT + 1)
        for d in range(2, KEPT):
            others = others + square_sum(i * KEPT + d)
        return total + own + 2.0 * others

    quartic = jnp.sum(lax.fori_loop(0, BLOCKS, squares, jnp.zeros((8, BLOCK), jnp.float32)))
    quartic = jnp.full((1, 1), quartic, jnp.float32)
    scale = 1.0 / jnp.sqrt(jnp.sqrt(quartic) + EPSILON)
    square = scale * scale

    def cut(j):
        return slice(j * BLOCK, (j + 1) * BLOCK)

    def into_product(j, total):
        product[:, cut(j)] = square * total

    def quintic(keep, finish):
        times_gram(gram_ref, value, into_product)
        value[...] = product[...].astype(jnp.bfloat16)
        times_gram(
            gram_ref,
            value,
            lambda j, total: finish(
                j,
                COEF_LINEAR * keep[:, cut(j)]
                + COEF_CUBIC * product[:, cut(j)]
                + COEF_QUINTIC * (square * total),
            ),
        )

    point[...] = base_ref[...].astype(jnp.float32) * scale
    value[...] = point[...].astype(jnp.bfloat16)

    def step(stage, _):
        def finish(j, total):
            point[:, cut(j)] = total

        quintic(point, finish)
        value[...] = point[...].astype(jnp.bfloat16)
        return 0

    step(0, 0)
    first = out_ref
    first[...] = COEF_LINEAR * point[...]

    def gram_of_second(number, _):
        coefficient = jnp.where(number == 0, COEF_CUBIC, COEF_QUINTIC)
        step(0, 0)
        times_gram(gram_ref, value, into_product)
        point[...] = product[...]
        value[...] = point[...].astype(jnp.bfloat16)
        step(0, 0)
        first[...] += coefficient * point[...]
        return 0

    lax.fori_loop(0, 2, gram_of_second, 0)


def newton_schulz(gram, base):
    return pl.pallas_call(
        newton_schulz_kernel,
        out_shape=jax.ShapeDtypeStruct((OWN_COLS, M), jnp.float32),
        in_specs=[pl.BlockSpec(memory_space=pltpu.VMEM)] * 2,
        out_specs=pl.BlockSpec(memory_space=pltpu.VMEM),
        scratch_shapes=[
            pltpu.VMEM((OWN_COLS, M), jnp.bfloat16),
            pltpu.VMEM((OWN_COLS, M), jnp.float32),
            pltpu.VMEM((OWN_COLS, M), jnp.float32),
        ],
        compiler_params=pltpu.CompilerParams(vmem_limit_bytes=48 * 2**20),
        name="newton_schulz",
    )(gram, base)


def per_device(gradient, momentum):
    grad32 = gradient.astype(jnp.float32)
    buffer = MOMENTUM_DECAY * momentum + grad32
    nesterov = grad32 + MOMENTUM_DECAY * buffer
    base = nesterov.astype(jnp.bfloat16)
    panel = lax.all_gather(base, "row", axis=0, tiled=True)
    units, columns = partial_gram(panel)
    shares = lax.psum_scatter(
        units, "col", scatter_dimension=0, axis_index_groups=X_GROUPS, tiled=True
    )
    shares = lax.psum_scatter(
        shares, "col", scatter_dimension=0, axis_index_groups=Z_GROUPS, tiled=True
    )
    gram = lax.all_gather(shares, ("row", "col"), axis=0, tiled=True)
    gram = gram.reshape(BLOCKS * KEPT, BLOCK, BLOCK)
    combined = newton_schulz(gram, columns)
    update = (combined * UPDATE_SCALE).astype(jnp.bfloat16)
    update = update.reshape(OWN_COLS, ROWS, OWN_ROWS).transpose(1, 0, 2)
    update = lax.all_to_all(update, "row", split_axis=0, concat_axis=0)
    update_matrix = update.reshape(PANEL_COLS, OWN_ROWS).T
    return (update_matrix, buffer)


def solution(mesh):
    return jax.shard_map(
        per_device,
        mesh=mesh,
        in_specs=(P("row", "col"), P("row", "col")),
        out_specs=(P("row", "col"), P("row", "col")),
        check_vma=False,
    )
```

```python
import math

import jax
import jax.numpy as jnp
from jax import lax
from jax.experimental import pallas as pl
from jax.experimental.pallas import tpu as pltpu
from jax.sharding import PartitionSpec as P

M = 3584
N = 12288
ROWS = 8
COLS = 32
X_CHIPS = 4
Y_CHIPS = 4
Z_CHIPS = 8
CORES = 2

MOMENTUM_DECAY = 0.95
EPSILON = 1e-07
COEF_LINEAR = 3.4445
COEF_CUBIC = -4.775
COEF_QUINTIC = 2.0315
UPDATE_SCALE = 0.2 * math.sqrt(max(M, N))

BLOCK = 512
BLOCKS = M // BLOCK
KEPT = (BLOCKS + 1) // 2
TILE = 256
TILES = BLOCKS * KEPT * 4
GRAM_ROWS = TILES * TILE
ROW_TILES = TILES // ROWS
PANEL_COLS = N // COLS
OWN_COLS = PANEL_COLS // ROWS
OWN_ROWS = M // ROWS
CHUNK = GRAM_ROWS // (ROWS * X_CHIPS)
SHARE = CHUNK // Z_CHIPS
HALF_CHUNK = CHUNK // 2
PIECE = TILE // 2
CHUNK_PIECES = CHUNK // PIECE
STEPS = 12

LINES = ((0, (0, 1, 2, 3)), (1, (0, 1, 2, 3)), (3, (0, 1, 2, 3)), (2, (0, 1)), (2, (2, 3)))
PARTS = [
    (half, [(last, k) if half == 0 else (k, last) for k in shifts], other_core)
    for other_core in (False, True)
    for half in (0, 1)
    for last, shifts in LINES
]

Z_GROUPS = [[x * Z_CHIPS + z for z in range(Z_CHIPS)] for x in range(X_CHIPS)]


def dot_nt(left, right):
    return lax.dot_general(
        left, right, (((1,), (1,)), ((), ())), preferred_element_type=jnp.float32
    )


def over_x(value, shift):
    pairs = [
        (x * Z_CHIPS + z, (x + shift) % X_CHIPS * Z_CHIPS + z)
        for x in range(X_CHIPS)
        for z in range(Z_CHIPS)
    ]
    return lax.ppermute(value, "col", pairs)


def over_y(value, shift):
    pairs = [
        (y * CORES + c, (y + shift) % Y_CHIPS * CORES + c)
        for y in range(Y_CHIPS)
        for c in range(CORES)
    ]
    return lax.ppermute(value, "row", pairs)


def over_cores(value):
    pairs = [
        (y * CORES + c, y * CORES + 1 - c) for y in range(Y_CHIPS) for c in range(CORES)
    ]
    return lax.ppermute(value, "row", pairs)


def over_z(value):
    return lax.all_to_all(
        value, "col", split_axis=0, concat_axis=0, axis_index_groups=Z_GROUPS
    )


def gram_kernel(panel_ref, *refs):
    chunk_refs, columns_ref = refs[:X_CHIPS], refs[X_CHIPS]
    row = lax.axis_index("row")
    x = lax.axis_index("col") // Z_CHIPS
    wanted = row * OWN_COLS + lax.broadcasted_iota(jnp.int32, (OWN_COLS, PANEL_COLS), 0)
    column = lax.broadcasted_iota(jnp.int32, (OWN_COLS, PANEL_COLS), 1)
    pick = jnp.where(wanted == column, 1.0, 0.0).astype(jnp.bfloat16)
    for shift in range(X_CHIPS):
        owner = lax.rem(x + shift, X_CHIPS)
        for k in range(CHUNK_PIECES):
            piece = owner * CHUNK_PIECES + k
            tile = row * ROW_TILES + piece // 2
            block = tile // 4
            i, d = block // KEPT, block % KEPT
            j = lax.rem(i + d, BLOCKS)
            top = i * BLOCK + tile % 4 // 2 * TILE + piece % 2 * PIECE
            across = j * BLOCK + tile % 2 * TILE
            left = panel_ref[pl.ds(pl.multiple_of(top, PIECE), PIECE), :]
            right = panel_ref[pl.ds(pl.multiple_of(across, TILE), TILE), :]
            chunk_refs[shift][k * PIECE : (k + 1) * PIECE, :] = dot_nt(left, right).astype(
                jnp.bfloat16
            )
    for b in range(BLOCKS):
        rows = panel_ref[b * BLOCK : (b + 1) * BLOCK, :]
        columns_ref[:, b * BLOCK : (b + 1) * BLOCK] = dot_nt(pick, rows).astype(jnp.bfloat16)


def partial_gram(panel):
    vmem = pl.BlockSpec(memory_space=pltpu.VMEM)
    outs = pl.pallas_call(
        gram_kernel,
        out_shape=[jax.ShapeDtypeStruct((CHUNK, TILE), jnp.bfloat16)] * X_CHIPS
        + [jax.ShapeDtypeStruct((OWN_COLS, M), jnp.bfloat16)],
        in_specs=[vmem],
        out_specs=[vmem] * (X_CHIPS + 1),
        compiler_params=pltpu.CompilerParams(vmem_limit_bytes=32 * 2**20),
        name="partial_gram",
    )(panel)
    return outs[:X_CHIPS], outs[X_CHIPS]


def tile_rows(i, d, half, column_half):
    start = (((i * KEPT + d) * 2 + half) * 2 + column_half) * TILE
    return pl.ds(start, TILE)


def mirror_rows(j, d, half, column_half):
    start = (((j * (KEPT - 1) + d - 1) * 2 + half) * 2 + column_half) * TILE
    return pl.ds(start, TILE)


def newton_schulz_kernel(base_ref, *refs):
    parts = refs[: len(PARTS)]
    out_ref, gram, mirror, value, state, total, sems = refs[len(PARTS) :]
    row = lax.axis_index("row")
    y, core = row // CORES, row % CORES
    x = lax.axis_index("col") // Z_CHIPS
    copies = []
    for part, (half, shifts, other_core) in zip(parts, PARTS):
        for k, (y_shift, x_shift) in enumerate(shifts):
            from_row = lax.rem(y + Y_CHIPS - y_shift, Y_CHIPS) * CORES
            from_row = from_row + (1 - core if other_core else core)
            from_x = lax.rem(x + X_CHIPS - x_shift, X_CHIPS)
            start = (from_row * X_CHIPS + from_x) * CHUNK + half * HALF_CHUNK
            copies.append(
                pltpu.make_async_copy(
                    part.at[k],
                    gram.at[pl.ds(pl.multiple_of(start, HALF_CHUNK), HALF_CHUNK), :],
                    sems.at[len(copies)],
                )
            )
    for copy in copies:
        copy.start()
    for copy in copies:
        copy.wait()

    one = lax.broadcasted_iota(jnp.int32, (TILE, TILE), 0)
    other = lax.broadcasted_iota(jnp.int32, (TILE, TILE), 1)
    identity = jnp.where(one == other, 1.0, 0.0).astype(jnp.bfloat16)

    def square_sum(tile):
        part = tile.astype(jnp.float32)
        return jnp.sum((part * part).reshape(TILE // 8, 8, TILE), axis=0)

    def prepare(i, sums):
        own, others = sums
        for half in range(2):
            for column_half in range(2):
                own = own + square_sum(gram[tile_rows(i, 0, half, column_half), :])
                for d in range(1, KEPT):
                    tile = gram[tile_rows(i, d, half, column_half), :]
                    others = others + square_sum(tile)
                    mirror[mirror_rows(i, d, half, column_half), :] = dot_nt(
                        identity, tile
                    ).astype(jnp.bfloat16)
        return own, others

    zeros = jnp.zeros((8, TILE), jnp.float32)
    own, others = lax.fori_loop(0, BLOCKS, prepare, (zeros, zeros))
    quartic = jnp.full((1, 1), jnp.sum(own + 2.0 * others), jnp.float32)
    scale = 1.0 / jnp.sqrt(jnp.sqrt(quartic) + EPSILON)
    square = scale * scale

    state[...] = base_ref[...].astype(jnp.float32) * scale
    value[0] = state[...].astype(jnp.bfloat16)

    def step(number, _):
        now = lax.rem(number, 2)
        place = jnp.where(number < 2, number, lax.rem(number + 3, 5))
        cubic = (place == 0) | (place == 3)
        quintic = (place == 1) | (place == 4)
        keep = jnp.where(cubic, COEF_LINEAR, jnp.where(quintic, 1.0, 0.0))
        add = jnp.where(cubic, COEF_CUBIC, jnp.where(quintic, COEF_QUINTIC, 1.0))
        from_product = jnp.where(cubic, 1.0, 0.0)
        from_state = jnp.where(cubic, 0.0, 1.0)
        for j in range(BLOCKS):
            for column_half in range(2):
                product = None
                for d in range(KEPT):
                    i = (j - d) % BLOCKS
                    for half in range(2):
                        term = jnp.dot(
                            value[now, :, pl.ds(i * BLOCK + half * TILE, TILE)],
                            gram[tile_rows(i, d, half, column_half), :],
                            preferred_element_type=jnp.float32,
                        )
                        product = term if product is None else product + term
                for d in range(1, KEPT):
                    i = (j + d) % BLOCKS
                    for half in range(2):
                        product = product + jnp.dot(
                            value[now, :, pl.ds(i * BLOCK + half * TILE, TILE)],
                            mirror[mirror_rows(j, d, column_half, half), :],
                            preferred_element_type=jnp.float32,
                        )
                cut = pl.ds(j * BLOCK + column_half * TILE, TILE)
                product = square * product
                result = keep * state[:, cut] + add * product
                state[:, cut] = result
                value[1 - now, :, cut] = (from_product * product + from_state * result).astype(
                    jnp.bfloat16
                )

        @pl.when(number == 1)
        def _():
            total[...] = COEF_LINEAR * state[...]

        @pl.when(number == 6)
        def _():
            total[...] += COEF_CUBIC * state[...]

        return 0

    lax.fori_loop(0, STEPS, step, 0)
    out_ref[...] = (UPDATE_SCALE * (total[...] + COEF_QUINTIC * state[...])).astype(jnp.bfloat16)


def newton_schulz(base, parts):
    mirror_tiles = BLOCKS * (KEPT - 1) * 4
    return pl.pallas_call(
        newton_schulz_kernel,
        out_shape=jax.ShapeDtypeStruct((OWN_COLS, M), jnp.bfloat16),
        in_specs=[pl.BlockSpec(memory_space=pltpu.VMEM)]
        + [pl.BlockSpec(memory_space=pl.ANY)] * len(parts),
        out_specs=pl.BlockSpec(memory_space=pltpu.VMEM),
        scratch_shapes=[
            pltpu.VMEM((GRAM_ROWS, TILE), jnp.bfloat16),
            pltpu.VMEM((mirror_tiles * TILE, TILE), jnp.bfloat16),
            pltpu.VMEM((2, OWN_COLS, M), jnp.bfloat16),
            pltpu.VMEM((OWN_COLS, M), jnp.float32),
            pltpu.VMEM((OWN_COLS, M), jnp.float32),
            pltpu.SemaphoreType.DMA((sum(len(shifts) for _, shifts, _ in PARTS),)),
        ],
        compiler_params=pltpu.CompilerParams(vmem_limit_bytes=48 * 2**20),
        name="newton_schulz",
    )(base, *parts)


def add_up(parts):
    total = parts[0].astype(jnp.float32)
    for part in parts[1:]:
        total = total + part.astype(jnp.float32)
    return total.astype(jnp.bfloat16)


def scattered_sum(chunks):
    received = [chunks[0]] + [over_x(chunks[k], k) for k in (2, 1, 3)]
    shares = over_z(add_up(received).reshape(Z_CHIPS, SHARE, TILE))
    return add_up([shares[z] for z in range(Z_CHIPS)])


def gathered(share):
    chunk = over_z(jnp.broadcast_to(share[None], (Z_CHIPS, SHARE, TILE))).reshape(CHUNK, TILE)
    first, second = chunk[:HALF_CHUNK], chunk[HALF_CHUNK:]
    from_x = {k: over_x(first, k) for k in (1, 3, 2)}
    from_y = {k: over_y(second, k) for k in (1, 3, 2)}
    first = jnp.stack([first] + [from_x[k] for k in (1, 2, 3)])
    second = jnp.stack([second] + [from_y[k] for k in (1, 2, 3)])
    first, second = lax.optimization_barrier((first, second))
    ups, downs = [over_y(first, 1), over_x(second, 1)], [over_y(first, 3), over_x(second, 3)]
    ups, downs = lax.optimization_barrier((ups, downs))
    parts = []
    for own, over, up, down in zip((first, second), (over_y, over_x), ups, downs):
        parts += [own, up, down, over(up[:2], 1), over(down[2:], 3)]
    return parts + [over_cores(part) for part in parts]


def per_device(gradient, momentum):
    grad32 = gradient.astype(jnp.float32)
    buffer = MOMENTUM_DECAY * momentum + grad32
    nesterov = grad32 + MOMENTUM_DECAY * buffer
    base = nesterov.astype(jnp.bfloat16)
    panel = lax.all_gather(base, "row", axis=0, tiled=True)
    chunks, columns = partial_gram(panel)
    parts = gathered(scattered_sum(chunks))
    update = newton_schulz(columns, parts)
    update = update.reshape(OWN_COLS, ROWS, OWN_ROWS).transpose(1, 0, 2)
    update = lax.all_to_all(update, "row", split_axis=0, concat_axis=0)
    update_matrix = update.reshape(PANEL_COLS, OWN_ROWS).T
    return (update_matrix, buffer)


def solution(mesh):
    return jax.shard_map(
        per_device,
        mesh=mesh,
        in_specs=(P("row", "col"), P("row", "col")),
        out_specs=(P("row", "col"), P("row", "col")),
        check_vma=False,
    )
```

```python
import math

import jax
import jax.numpy as jnp
from jax import lax
from jax.experimental import pallas as pl
from jax.experimental.pallas import tpu as pltpu
from jax.sharding import PartitionSpec as P

M = 3584
N = 12288
ROWS = 8
COLS = 32
X_CHIPS = 4
Y_CHIPS = 4
Z_CHIPS = 8
CORES = 2

MOMENTUM_DECAY = 0.95
EPSILON = 1e-07
COEF_LINEAR = 3.4445
COEF_CUBIC = -4.775
COEF_QUINTIC = 2.0315
UPDATE_SCALE = 0.2 * math.sqrt(max(M, N))

BLOCK = 512
BLOCKS = M // BLOCK
KEPT = (BLOCKS + 1) // 2
TILE = 256
TILES = BLOCKS * KEPT * 4
GRAM_ROWS = TILES * TILE
ROW_TILES = TILES // ROWS
PANEL_COLS = N // COLS
OWN_COLS = PANEL_COLS // ROWS
OWN_ROWS = M // ROWS
CHUNK = GRAM_ROWS // (ROWS * X_CHIPS)
SHARE = CHUNK // Z_CHIPS
HALF_CHUNK = CHUNK // 2
PIECE = TILE // 2
CHUNK_PIECES = CHUNK // PIECE
STEPS = 12
STRIP = M // 4

LINES = ((0, (0, 1, 2, 3)), (1, (0, 1, 2, 3)), (3, (0, 1, 2, 3)), (2, (0, 1)), (2, (2, 3)))
PARTS = [
    (half, [(last, k) if half == 0 else (k, last) for k in shifts], other_core)
    for other_core in (False, True)
    for half in (0, 1)
    for last, shifts in LINES
]

Z_GROUPS = [[x * Z_CHIPS + z for z in range(Z_CHIPS)] for x in range(X_CHIPS)]


def dot_nt(left, right):
    return lax.dot_general(
        left, right, (((1,), (1,)), ((), ())), preferred_element_type=jnp.float32
    )


def over_x(value, shift):
    pairs = [
        (x * Z_CHIPS + z, (x + shift) % X_CHIPS * Z_CHIPS + z)
        for x in range(X_CHIPS)
        for z in range(Z_CHIPS)
    ]
    return lax.ppermute(value, "col", pairs)


def over_y(value, shift):
    pairs = [
        (y * CORES + c, (y + shift) % Y_CHIPS * CORES + c)
        for y in range(Y_CHIPS)
        for c in range(CORES)
    ]
    return lax.ppermute(value, "row", pairs)


def over_cores(value):
    pairs = [
        (y * CORES + c, y * CORES + 1 - c) for y in range(Y_CHIPS) for c in range(CORES)
    ]
    return lax.ppermute(value, "row", pairs)


def over_z(value):
    return lax.all_to_all(
        value, "col", split_axis=0, concat_axis=0, axis_index_groups=Z_GROUPS
    )


def gram_kernel(*refs):
    row_refs, refs = refs[:ROWS], refs[ROWS:]
    chunk_refs, (columns_ref, panel_ref, sems) = refs[:X_CHIPS], refs[X_CHIPS:]
    row = lax.axis_index("row")
    y, core = row // CORES, row % CORES
    copies = []
    for number, row_ref in enumerate(row_refs):
        shift, c = number % Y_CHIPS, core if number < Y_CHIPS else 1 - core
        owner = lax.rem(y + Y_CHIPS - shift, Y_CHIPS) * CORES + c
        copies.append(
            pltpu.make_async_copy(
                row_ref,
                panel_ref.at[pl.ds(pl.multiple_of(owner * OWN_ROWS, OWN_ROWS), OWN_ROWS), :],
                sems.at[number],
            )
        )
    for copy in copies:
        copy.start()
    for copy in copies:
        copy.wait()
    x = lax.axis_index("col") // Z_CHIPS
    wanted = row * OWN_COLS + lax.broadcasted_iota(jnp.int32, (OWN_COLS, PANEL_COLS), 0)
    column = lax.broadcasted_iota(jnp.int32, (OWN_COLS, PANEL_COLS), 1)
    pick = jnp.where(wanted == column, 1.0, 0.0).astype(jnp.bfloat16)
    for shift in range(X_CHIPS):
        owner = lax.rem(x + shift, X_CHIPS)
        for k in range(CHUNK_PIECES):
            piece = owner * CHUNK_PIECES + k
            tile = row * ROW_TILES + piece // 2
            block = tile // 4
            i, d = block // KEPT, block % KEPT
            j = lax.rem(i + d, BLOCKS)
            top = i * BLOCK + tile % 4 // 2 * TILE + piece % 2 * PIECE
            across = j * BLOCK + tile % 2 * TILE
            left = panel_ref[pl.ds(pl.multiple_of(top, PIECE), PIECE), :]
            right = panel_ref[pl.ds(pl.multiple_of(across, TILE), TILE), :]
            chunk_refs[shift][k * PIECE : (k + 1) * PIECE, :] = dot_nt(left, right).astype(
                jnp.bfloat16
            )
    for b in range(BLOCKS):
        rows = panel_ref[b * BLOCK : (b + 1) * BLOCK, :]
        columns_ref[:, b * BLOCK : (b + 1) * BLOCK] = dot_nt(pick, rows).astype(jnp.bfloat16)


def partial_gram(rows):
    vmem = pl.BlockSpec(memory_space=pltpu.VMEM)
    outs = pl.pallas_call(
        gram_kernel,
        out_shape=[jax.ShapeDtypeStruct((CHUNK, TILE), jnp.bfloat16)] * X_CHIPS
        + [jax.ShapeDtypeStruct((OWN_COLS, M), jnp.bfloat16)],
        in_specs=[pl.BlockSpec(memory_space=pl.ANY)] * ROWS,
        out_specs=[vmem] * (X_CHIPS + 1),
        scratch_shapes=[
            pltpu.VMEM((M, PANEL_COLS), jnp.bfloat16),
            pltpu.SemaphoreType.DMA((ROWS,)),
        ],
        compiler_params=pltpu.CompilerParams(vmem_limit_bytes=16 * 2**20),
        name="partial_gram",
    )(*rows)
    return outs[:X_CHIPS], outs[X_CHIPS]


def tile_rows(i, d, half, column_half):
    start = (((i * KEPT + d) * 2 + half) * 2 + column_half) * TILE
    return pl.ds(start, TILE)


def newton_schulz_kernel(base_ref, *refs):
    parts = refs[: len(PARTS)]
    out_ref, tiles, gram, value, state, total, sems = refs[len(PARTS) :]
    row = lax.axis_index("row")
    y, core = row // CORES, row % CORES
    x = lax.axis_index("col") // Z_CHIPS
    copies = []
    for part, (half, shifts, other_core) in zip(parts, PARTS):
        for k, (y_shift, x_shift) in enumerate(shifts):
            from_row = lax.rem(y + Y_CHIPS - y_shift, Y_CHIPS) * CORES
            from_row = from_row + (1 - core if other_core else core)
            from_x = lax.rem(x + X_CHIPS - x_shift, X_CHIPS)
            start = (from_row * X_CHIPS + from_x) * CHUNK + half * HALF_CHUNK
            copies.append(
                pltpu.make_async_copy(
                    part.at[k],
                    tiles.at[pl.ds(pl.multiple_of(start, HALF_CHUNK), HALF_CHUNK), :],
                    sems.at[len(copies)],
                )
            )
    for copy in copies:
        copy.start()
    for copy in copies:
        copy.wait()

    one = lax.broadcasted_iota(jnp.int32, (TILE, TILE), 0)
    other = lax.broadcasted_iota(jnp.int32, (TILE, TILE), 1)
    identity = jnp.where(one == other, 1.0, 0.0).astype(jnp.bfloat16)

    def square_sum(tile):
        part = tile.astype(jnp.float32)
        return jnp.sum((part * part).reshape(TILE // 8, 8, TILE), axis=0)

    own = others = jnp.zeros((8, TILE), jnp.float32)
    for i in range(BLOCKS):
        for d in range(KEPT):
            j = (i + d) % BLOCKS
            for half in range(2):
                down = pl.ds(i * BLOCK + half * TILE, TILE)
                for column_half in range(2):
                    across = pl.ds(j * BLOCK + column_half * TILE, TILE)
                    tile = tiles[tile_rows(i, d, half, column_half), :]
                    gram[down, across] = tile
                    if d == 0:
                        own = own + square_sum(tile)
                    else:
                        others = others + square_sum(tile)
                        gram[across, down] = dot_nt(identity, tile).astype(jnp.bfloat16)
    quartic = jnp.full((1, 1), jnp.sum(own + 2.0 * others), jnp.float32)
    scale = 1.0 / jnp.sqrt(jnp.sqrt(quartic) + EPSILON)
    square = scale * scale

    state[...] = base_ref[...].astype(jnp.float32) * scale
    value[0] = state[...].astype(jnp.bfloat16)

    def step(number, _):
        now = lax.rem(number, 2)
        place = jnp.where(number < 2, number, lax.rem(number + 3, 5))
        cubic = (place == 0) | (place == 3)
        quintic = (place == 1) | (place == 4)
        keep = jnp.where(cubic, COEF_LINEAR, jnp.where(quintic, 1.0, 0.0))
        add = jnp.where(cubic, COEF_CUBIC, jnp.where(quintic, COEF_QUINTIC, 1.0))
        from_product = jnp.where(cubic, 1.0, 0.0)
        from_state = jnp.where(cubic, 0.0, 1.0)
        for strip in range(M // STRIP):
            cut = pl.ds(strip * STRIP, STRIP)
            product = square * jnp.dot(
                value[now], gram[:, cut], preferred_element_type=jnp.float32
            )
            result = keep * state[:, cut] + add * product
            state[:, cut] = result
            value[1 - now, :, cut] = (from_product * product + from_state * result).astype(
                jnp.bfloat16
            )

        @pl.when(number == 1)
        def _():
            total[...] = COEF_LINEAR * state[...]

        @pl.when(number == 6)
        def _():
            total[...] += COEF_CUBIC * state[...]

        return 0

    lax.fori_loop(0, STEPS, step, 0)
    out_ref[...] = (UPDATE_SCALE * (total[...] + COEF_QUINTIC * state[...])).astype(jnp.bfloat16)


def newton_schulz(base, parts):
    return pl.pallas_call(
        newton_schulz_kernel,
        out_shape=jax.ShapeDtypeStruct((OWN_COLS, M), jnp.bfloat16),
        in_specs=[pl.BlockSpec(memory_space=pltpu.VMEM)]
        + [pl.BlockSpec(memory_space=pl.ANY)] * len(parts),
        out_specs=pl.BlockSpec(memory_space=pltpu.VMEM),
        scratch_shapes=[
            pltpu.VMEM((GRAM_ROWS, TILE), jnp.bfloat16),
            pltpu.VMEM((M, M), jnp.bfloat16),
            pltpu.VMEM((2, OWN_COLS, M), jnp.bfloat16),
            pltpu.VMEM((OWN_COLS, M), jnp.float32),
            pltpu.VMEM((OWN_COLS, M), jnp.float32),
            pltpu.SemaphoreType.DMA((sum(len(shifts) for _, shifts, _ in PARTS),)),
        ],
        compiler_params=pltpu.CompilerParams(vmem_limit_bytes=43 * 2**20),
        name="newton_schulz",
    )(base, *parts)


def add_up(parts):
    total = parts[0].astype(jnp.float32)
    for part in parts[1:]:
        total = total + part.astype(jnp.float32)
    return total.astype(jnp.bfloat16)


def scattered_sum(chunks):
    received = [chunks[0]] + [over_x(chunks[k], k) for k in (2, 1, 3)]
    shares = over_z(add_up(received).reshape(Z_CHIPS, SHARE, TILE))
    return add_up([shares[z] for z in range(Z_CHIPS)])


def gathered(share):
    chunk = over_z(jnp.broadcast_to(share[None], (Z_CHIPS, SHARE, TILE))).reshape(CHUNK, TILE)
    first, second = chunk[:HALF_CHUNK], chunk[HALF_CHUNK:]
    from_x = {k: over_x(first, k) for k in (1, 3, 2)}
    from_y = {k: over_y(second, k) for k in (1, 3, 2)}
    first = jnp.stack([first] + [from_x[k] for k in (1, 2, 3)])
    second = jnp.stack([second] + [from_y[k] for k in (1, 2, 3)])
    first, second = lax.optimization_barrier((first, second))
    ups, downs = [over_y(first, 1), over_x(second, 1)], [over_y(first, 3), over_x(second, 3)]
    ups, downs = lax.optimization_barrier((ups, downs))
    parts = []
    for own, over, up, down in zip((first, second), (over_y, over_x), ups, downs):
        parts += [own, up, down, over(up[:2], 1), over(down[2:], 3)]
    return parts + [over_cores(part) for part in parts]


def per_device(gradient, momentum):
    grad32 = gradient.astype(jnp.float32)
    buffer = MOMENTUM_DECAY * momentum + grad32
    nesterov = grad32 + MOMENTUM_DECAY * buffer
    base = nesterov.astype(jnp.bfloat16)
    shifted = {k: over_y(base, k) for k in (1, 3, 2)}
    rows = [base] + [shifted[k] for k in (1, 2, 3)]
    chunks, columns = partial_gram(rows + [over_cores(part) for part in rows])
    parts = gathered(scattered_sum(chunks))
    update = newton_schulz(columns, parts)
    update = update.reshape(OWN_COLS, ROWS, OWN_ROWS).transpose(1, 0, 2)
    update = lax.all_to_all(update, "row", split_axis=0, concat_axis=0)
    update_matrix = update.reshape(PANEL_COLS, OWN_ROWS).T
    return (update_matrix, buffer)


def solution(mesh):
    return jax.shard_map(
        per_device,
        mesh=mesh,
        in_specs=(P("row", "col"), P("row", "col")),
        out_specs=(P("row", "col"), P("row", "col")),
        check_vma=False,
    )
```

```python
import math

import jax
import jax.numpy as jnp
from jax import lax
from jax.experimental import pallas as pl
from jax.experimental.pallas import tpu as pltpu
from jax.sharding import PartitionSpec as P

M = 3584
N = 12288
ROWS = 8
COLS = 32
X_CHIPS = 4
Y_CHIPS = 4
Z_CHIPS = 8
CORES = 2

MOMENTUM_DECAY = 0.95
EPSILON = 1e-07
COEF_LINEAR = 3.4445
COEF_CUBIC = -4.775
COEF_QUINTIC = 2.0315
UPDATE_SCALE = 0.2 * math.sqrt(max(M, N))

BLOCK = 512
BLOCKS = M // BLOCK
KEPT = (BLOCKS + 1) // 2
TILE = 256
TILES = BLOCKS * KEPT * 4
GRAM_ROWS = TILES * TILE
ROW_TILES = TILES // ROWS
PANEL_COLS = N // COLS
OWN_COLS = PANEL_COLS // ROWS
OWN_ROWS = M // ROWS
CHUNK = GRAM_ROWS // (ROWS * X_CHIPS)
SHARE = CHUNK // Z_CHIPS
HALF_CHUNK = CHUNK // 2
PIECE = TILE // 2
CHUNK_PIECES = CHUNK // PIECE
STEPS = 12
STRIP = M // 4

LINES = ((0, (0, 1, 2, 3)), (1, (0, 1, 2, 3)), (3, (0, 1, 2, 3)), (2, (0, 1)), (2, (2, 3)))
PARTS = [
    (half, [(last, k) if half == 0 else (k, last) for k in shifts], other_core)
    for other_core in (False, True)
    for half in (0, 1)
    for last, shifts in LINES
]

Z_GROUPS = [[x * Z_CHIPS + z for z in range(Z_CHIPS)] for x in range(X_CHIPS)]


def dot_nt(left, right):
    return lax.dot_general(
        left, right, (((1,), (1,)), ((), ())), preferred_element_type=jnp.float32
    )


def over_x(value, shift):
    pairs = [
        (x * Z_CHIPS + z, (x + shift) % X_CHIPS * Z_CHIPS + z)
        for x in range(X_CHIPS)
        for z in range(Z_CHIPS)
    ]
    return lax.ppermute(value, "col", pairs)


def over_y(value, shift):
    pairs = [
        (y * CORES + c, (y + shift) % Y_CHIPS * CORES + c)
        for y in range(Y_CHIPS)
        for c in range(CORES)
    ]
    return lax.ppermute(value, "row", pairs)


def over_cores(value):
    pairs = [
        (y * CORES + c, y * CORES + 1 - c) for y in range(Y_CHIPS) for c in range(CORES)
    ]
    return lax.ppermute(value, "row", pairs)


def over_z(value):
    return lax.all_to_all(
        value, "col", split_axis=0, concat_axis=0, axis_index_groups=Z_GROUPS
    )


def gram_kernel(*refs):
    row_refs, refs = refs[:ROWS], refs[ROWS:]
    chunk_refs, (columns_ref, panel_ref, sems) = refs[:X_CHIPS], refs[X_CHIPS:]
    row = lax.axis_index("row")
    y, core = row // CORES, row % CORES
    copies = []
    for number, row_ref in enumerate(row_refs):
        shift, c = number % Y_CHIPS, core if number < Y_CHIPS else 1 - core
        owner = lax.rem(y + Y_CHIPS - shift, Y_CHIPS) * CORES + c
        copies.append(
            pltpu.make_async_copy(
                row_ref,
                panel_ref.at[pl.ds(pl.multiple_of(owner * OWN_ROWS, OWN_ROWS), OWN_ROWS), :],
                sems.at[number],
            )
        )
    for copy in copies:
        copy.start()
    for copy in copies:
        copy.wait()
    x = lax.axis_index("col") // Z_CHIPS
    wanted = row * OWN_COLS + lax.broadcasted_iota(jnp.int32, (OWN_COLS, PANEL_COLS), 0)
    column = lax.broadcasted_iota(jnp.int32, (OWN_COLS, PANEL_COLS), 1)
    pick = jnp.where(wanted == column, 1.0, 0.0).astype(jnp.bfloat16)
    for shift in range(X_CHIPS):
        owner = lax.rem(x + shift, X_CHIPS)
        for k in range(CHUNK_PIECES):
            piece = owner * CHUNK_PIECES + k
            tile = row * ROW_TILES + piece // 2
            block = tile // 4
            i, d = block // KEPT, block % KEPT
            j = lax.rem(i + d, BLOCKS)
            top = i * BLOCK + tile % 4 // 2 * TILE + piece % 2 * PIECE
            across = j * BLOCK + tile % 2 * TILE
            left = panel_ref[pl.ds(pl.multiple_of(top, PIECE), PIECE), :]
            right = panel_ref[pl.ds(pl.multiple_of(across, TILE), TILE), :]
            chunk_refs[shift][k * PIECE : (k + 1) * PIECE, :] = dot_nt(left, right).astype(
                jnp.bfloat16
            )
    for b in range(BLOCKS):
        rows = panel_ref[b * BLOCK : (b + 1) * BLOCK, :]
        columns_ref[:, b * BLOCK : (b + 1) * BLOCK] = dot_nt(pick, rows).astype(jnp.bfloat16)


def partial_gram(rows):
    vmem = pl.BlockSpec(memory_space=pltpu.VMEM)
    outs = pl.pallas_call(
        gram_kernel,
        out_shape=[jax.ShapeDtypeStruct((CHUNK, TILE), jnp.bfloat16)] * X_CHIPS
        + [jax.ShapeDtypeStruct((OWN_COLS, M), jnp.bfloat16)],
        in_specs=[pl.BlockSpec(memory_space=pl.ANY)] * ROWS,
        out_specs=[vmem] * (X_CHIPS + 1),
        scratch_shapes=[
            pltpu.VMEM((M, PANEL_COLS), jnp.bfloat16),
            pltpu.SemaphoreType.DMA((ROWS,)),
        ],
        compiler_params=pltpu.CompilerParams(vmem_limit_bytes=16 * 2**20),
        name="partial_gram",
    )(*rows)
    return outs[:X_CHIPS], outs[X_CHIPS]


def tile_rows(i, d, half, column_half):
    start = (((i * KEPT + d) * 2 + half) * 2 + column_half) * TILE
    return pl.ds(start, TILE)


def newton_schulz_kernel(base_ref, *refs):
    parts = refs[: len(PARTS)]
    out_ref, tiles, gram, value, state, total, sems = refs[len(PARTS) :]
    row = lax.axis_index("row")
    y, core = row // CORES, row % CORES
    x = lax.axis_index("col") // Z_CHIPS
    copies = []
    for part, (half, shifts, other_core) in zip(parts, PARTS):
        for k, (y_shift, x_shift) in enumerate(shifts):
            from_row = lax.rem(y + Y_CHIPS - y_shift, Y_CHIPS) * CORES
            from_row = from_row + (1 - core if other_core else core)
            from_x = lax.rem(x + X_CHIPS - x_shift, X_CHIPS)
            start = (from_row * X_CHIPS + from_x) * CHUNK + half * HALF_CHUNK
            copies.append(
                pltpu.make_async_copy(
                    part.at[k],
                    tiles.at[pl.ds(pl.multiple_of(start, HALF_CHUNK), HALF_CHUNK), :],
                    sems.at[len(copies)],
                )
            )
    for copy in copies:
        copy.start()
    for copy in copies:
        copy.wait()

    one = lax.broadcasted_iota(jnp.int32, (TILE, TILE), 0)
    other = lax.broadcasted_iota(jnp.int32, (TILE, TILE), 1)
    identity = jnp.where(one == other, 1.0, 0.0).astype(jnp.bfloat16)

    def square_sum(tile):
        part = tile.astype(jnp.float32)
        return jnp.sum((part * part).reshape(TILE // 8, 8, TILE), axis=0)

    own = others = jnp.zeros((8, TILE), jnp.float32)
    for i in range(BLOCKS):
        for d in range(KEPT):
            j = (i + d) % BLOCKS
            for half in range(2):
                down = pl.ds(i * BLOCK + half * TILE, TILE)
                for column_half in range(2):
                    across = pl.ds(j * BLOCK + column_half * TILE, TILE)
                    tile = tiles[tile_rows(i, d, half, column_half), :]
                    gram[down, across] = tile
                    if d == 0:
                        own = own + square_sum(tile)
                    else:
                        others = others + square_sum(tile)
                        gram[across, down] = dot_nt(identity, tile).astype(jnp.bfloat16)
    quartic = jnp.full((1, 1), jnp.sum(own + 2.0 * others), jnp.float32)
    scale = 1.0 / jnp.sqrt(jnp.sqrt(quartic) + EPSILON)
    square = scale * scale

    state[...] = base_ref[...].astype(jnp.float32) * scale
    value[0] = state[...].astype(jnp.bfloat16)

    def step(number, _):
        now = lax.rem(number, 2)
        place = jnp.where(number < 2, number, lax.rem(number + 3, 5))
        cubic = (place == 0) | (place == 3)
        quintic = (place == 1) | (place == 4)
        keep = jnp.where(cubic, COEF_LINEAR, jnp.where(quintic, 1.0, 0.0))
        add = jnp.where(cubic, COEF_CUBIC, jnp.where(quintic, COEF_QUINTIC, 1.0))
        from_product = jnp.where(cubic, 1.0, 0.0)
        from_state = jnp.where(cubic, 0.0, 1.0)
        for strip in range(M // STRIP):
            cut = pl.ds(strip * STRIP, STRIP)
            product = square * jnp.dot(
                value[now], gram[:, cut], preferred_element_type=jnp.float32
            )
            result = keep * state[:, cut] + add * product
            state[:, cut] = result
            value[1 - now, :, cut] = (from_product * product + from_state * result).astype(
                jnp.bfloat16
            )

        @pl.when(number == 1)
        def _():
            total[...] = COEF_LINEAR * state[...]

        @pl.when(number == 6)
        def _():
            total[...] += COEF_CUBIC * state[...]

        return 0

    lax.fori_loop(0, STEPS, step, 0)
    out_ref[...] = (UPDATE_SCALE * (total[...] + COEF_QUINTIC * state[...])).astype(jnp.bfloat16)


def newton_schulz(base, parts):
    return pl.pallas_call(
        newton_schulz_kernel,
        out_shape=jax.ShapeDtypeStruct((OWN_COLS, M), jnp.bfloat16),
        in_specs=[pl.BlockSpec(memory_space=pltpu.VMEM)]
        + [pl.BlockSpec(memory_space=pl.ANY)] * len(parts),
        out_specs=pl.BlockSpec(memory_space=pltpu.VMEM),
        scratch_shapes=[
            pltpu.VMEM((GRAM_ROWS, TILE), jnp.bfloat16),
            pltpu.VMEM((M, M), jnp.bfloat16),
            pltpu.VMEM((2, OWN_COLS, M), jnp.bfloat16),
            pltpu.VMEM((OWN_COLS, M), jnp.float32),
            pltpu.VMEM((OWN_COLS, M), jnp.float32),
            pltpu.SemaphoreType.DMA((sum(len(shifts) for _, shifts, _ in PARTS),)),
        ],
        compiler_params=pltpu.CompilerParams(vmem_limit_bytes=58 * 2**20),
        name="newton_schulz",
    )(base, *parts)


def add_up(parts):
    total = parts[0].astype(jnp.float32)
    for part in parts[1:]:
        total = total + part.astype(jnp.float32)
    return total.astype(jnp.bfloat16)


def scattered_sum(chunks):
    received = [chunks[0]] + [over_x(chunks[k], k) for k in (2, 1, 3)]
    shares = over_z(add_up(received).reshape(Z_CHIPS, SHARE, TILE))
    return add_up([shares[z] for z in range(Z_CHIPS)])


def gathered(share):
    chunk = over_z(jnp.broadcast_to(share[None], (Z_CHIPS, SHARE, TILE))).reshape(CHUNK, TILE)
    first, second = chunk[:HALF_CHUNK], chunk[HALF_CHUNK:]
    from_x = {k: over_x(first, k) for k in (1, 3, 2)}
    from_y = {k: over_y(second, k) for k in (1, 3, 2)}
    first = jnp.stack([first] + [from_x[k] for k in (1, 2, 3)])
    second = jnp.stack([second] + [from_y[k] for k in (1, 2, 3)])
    first, second = lax.optimization_barrier((first, second))
    ups, downs = [over_y(first, 1), over_x(second, 1)], [over_y(first, 3), over_x(second, 3)]
    swapped = [over_cores(first), over_cores(second)]
    onward = [up[:2] for up in ups], [down[2:] for down in downs]
    ups, downs, onward, swapped = lax.optimization_barrier((ups, downs, onward, swapped))
    own_core, other_core = [], []
    far = [[over(up, 1), over(down, 3)] for over, up, down in zip((over_y, over_x), *onward)]
    for own, swap, up, down, rest in zip((first, second), swapped, ups, downs, far):
        own_core += [own, up, down] + rest
        other_core += [swap] + [over_cores(part) for part in [up, down] + rest]
    return own_core + other_core


def per_device(gradient, momentum):
    grad32 = gradient.astype(jnp.float32)
    buffer = MOMENTUM_DECAY * momentum + grad32
    nesterov = grad32 + MOMENTUM_DECAY * buffer
    base = nesterov.astype(jnp.bfloat16)
    shifted = {k: over_y(base, k) for k in (1, 3, 2)}
    rows = [base] + [shifted[k] for k in (1, 2, 3)]
    chunks, columns = partial_gram(rows + [over_cores(part) for part in rows])
    parts = gathered(scattered_sum(chunks))
    update = newton_schulz(columns, parts)
    update = update.reshape(OWN_COLS, ROWS, OWN_ROWS).transpose(1, 0, 2)
    update = lax.all_to_all(update, "row", split_axis=0, concat_axis=0)
    update_matrix = update.reshape(PANEL_COLS, OWN_ROWS).T
    return (update_matrix, buffer)


def solution(mesh):
    return jax.shard_map(
        per_device,
        mesh=mesh,
        in_specs=(P("row", "col"), P("row", "col")),
        out_specs=(P("row", "col"), P("row", "col")),
        check_vma=False,
    )
```

```python
import math

import jax
import jax.numpy as jnp
from jax import lax
from jax.experimental import pallas as pl
from jax.experimental.pallas import tpu as pltpu
from jax.sharding import PartitionSpec as P

M = 3584
N = 12288
ROWS = 8
COLS = 32
X_CHIPS = 4
Y_CHIPS = 4
Z_CHIPS = 8
CORES = 2

MOMENTUM_DECAY = 0.95
EPSILON = 1e-07
COEF_LINEAR = 3.4445
COEF_CUBIC = -4.775
COEF_QUINTIC = 2.0315
UPDATE_SCALE = 0.2 * math.sqrt(max(M, N))

BLOCK = 512
BLOCKS = M // BLOCK
KEPT = (BLOCKS + 1) // 2
TILE = 256
TILES = BLOCKS * KEPT * 4
GRAM_ROWS = TILES * TILE
ROW_TILES = TILES // ROWS
PANEL_COLS = N // COLS
OWN_COLS = PANEL_COLS // ROWS
OWN_ROWS = M // ROWS
CHUNK = GRAM_ROWS // (ROWS * X_CHIPS)
SHARE = CHUNK // Z_CHIPS
HALF_CHUNK = CHUNK // 2
PIECE = TILE // 2
CHUNK_PIECES = CHUNK // PIECE
STEPS = 12
STRIP = M // 4

ALL_FOUR = (0, 1, 2, 3)


def line(half, last, others):
    return [(half, last, k) if half == 0 else (half, k, last) for k in others]


NEAR = [line(half, last, ALL_FOUR) for last in (0, 1, 3) for half in (0, 1)]
FAR = [line(half, 2, others) for half in (0, 1) for others in ((0, 1), (2, 3))]
OWN_PARTS = len(NEAR) + len(FAR)
PARTS = NEAR + FAR + [sum(NEAR[:2], []), sum(NEAR[2:], [])] + FAR

Z_GROUPS = [[x * Z_CHIPS + z for z in range(Z_CHIPS)] for x in range(X_CHIPS)]


def dot_nt(left, right):
    return lax.dot_general(
        left, right, (((1,), (1,)), ((), ())), preferred_element_type=jnp.float32
    )


def over_x(value, shift):
    pairs = [
        (x * Z_CHIPS + z, (x + shift) % X_CHIPS * Z_CHIPS + z)
        for x in range(X_CHIPS)
        for z in range(Z_CHIPS)
    ]
    return lax.ppermute(value, "col", pairs)


def over_y(value, shift):
    pairs = [
        (y * CORES + c, (y + shift) % Y_CHIPS * CORES + c)
        for y in range(Y_CHIPS)
        for c in range(CORES)
    ]
    return lax.ppermute(value, "row", pairs)


def over_cores(value):
    pairs = [
        (y * CORES + c, y * CORES + 1 - c) for y in range(Y_CHIPS) for c in range(CORES)
    ]
    return lax.ppermute(value, "row", pairs)


def over_z(value):
    return lax.all_to_all(
        value, "col", split_axis=0, concat_axis=0, axis_index_groups=Z_GROUPS
    )


def gram_kernel(*refs):
    row_refs, refs = refs[:ROWS], refs[ROWS:]
    chunk_refs, (columns_ref, panel_ref, sems) = refs[:X_CHIPS], refs[X_CHIPS:]
    row = lax.axis_index("row")
    y, core = row // CORES, row % CORES
    copies = []
    for number, row_ref in enumerate(row_refs):
        shift, c = number % Y_CHIPS, core if number < Y_CHIPS else 1 - core
        owner = lax.rem(y + Y_CHIPS - shift, Y_CHIPS) * CORES + c
        copies.append(
            pltpu.make_async_copy(
                row_ref,
                panel_ref.at[pl.ds(pl.multiple_of(owner * OWN_ROWS, OWN_ROWS), OWN_ROWS), :],
                sems.at[number],
            )
        )
    for copy in copies:
        copy.start()
    for copy in copies:
        copy.wait()
    x = lax.axis_index("col") // Z_CHIPS
    wanted = row * OWN_COLS + lax.broadcasted_iota(jnp.int32, (OWN_COLS, PANEL_COLS), 0)
    column = lax.broadcasted_iota(jnp.int32, (OWN_COLS, PANEL_COLS), 1)
    pick = jnp.where(wanted == column, 1.0, 0.0).astype(jnp.bfloat16)
    for shift in range(X_CHIPS):
        owner = lax.rem(x + shift, X_CHIPS)
        for k in range(CHUNK_PIECES):
            piece = owner * CHUNK_PIECES + k
            tile = row * ROW_TILES + piece // 2
            block = tile // 4
            i, d = block // KEPT, block % KEPT
            j = lax.rem(i + d, BLOCKS)
            top = i * BLOCK + tile % 4 // 2 * TILE + piece % 2 * PIECE
            across = j * BLOCK + tile % 2 * TILE
            left = panel_ref[pl.ds(pl.multiple_of(top, PIECE), PIECE), :]
            right = panel_ref[pl.ds(pl.multiple_of(across, TILE), TILE), :]
            chunk_refs[shift][k * PIECE : (k + 1) * PIECE, :] = dot_nt(left, right).astype(
                jnp.bfloat16
            )
    for b in range(BLOCKS):
        rows = panel_ref[b * BLOCK : (b + 1) * BLOCK, :]
        columns_ref[:, b * BLOCK : (b + 1) * BLOCK] = dot_nt(pick, rows).astype(jnp.bfloat16)


def partial_gram(rows):
    vmem = pl.BlockSpec(memory_space=pltpu.VMEM)
    outs = pl.pallas_call(
        gram_kernel,
        out_shape=[jax.ShapeDtypeStruct((CHUNK, TILE), jnp.bfloat16)] * X_CHIPS
        + [jax.ShapeDtypeStruct((OWN_COLS, M), jnp.bfloat16)],
        in_specs=[pl.BlockSpec(memory_space=pl.ANY)] * ROWS,
        out_specs=[vmem] * (X_CHIPS + 1),
        scratch_shapes=[
            pltpu.VMEM((M, PANEL_COLS), jnp.bfloat16),
            pltpu.SemaphoreType.DMA((ROWS,)),
        ],
        compiler_params=pltpu.CompilerParams(vmem_limit_bytes=16 * 2**20),
        name="partial_gram",
    )(*rows)
    return outs[:X_CHIPS], outs[X_CHIPS]


def tile_rows(i, d, half, column_half):
    start = (((i * KEPT + d) * 2 + half) * 2 + column_half) * TILE
    return pl.ds(start, TILE)


def newton_schulz_kernel(base_ref, *refs):
    parts = refs[: len(PARTS)]
    out_ref, tiles, gram, value, state, total, sems = refs[len(PARTS) :]
    row = lax.axis_index("row")
    y, core = row // CORES, row % CORES
    x = lax.axis_index("col") // Z_CHIPS
    copies = []
    for number, (part, places) in enumerate(zip(parts, PARTS)):
        from_core = core if number < OWN_PARTS else 1 - core
        for k, (half, y_shift, x_shift) in enumerate(places):
            from_row = lax.rem(y + Y_CHIPS - y_shift, Y_CHIPS) * CORES + from_core
            from_x = lax.rem(x + X_CHIPS - x_shift, X_CHIPS)
            start = (from_row * X_CHIPS + from_x) * CHUNK + half * HALF_CHUNK
            copies.append(
                pltpu.make_async_copy(
                    part.at[k],
                    tiles.at[pl.ds(pl.multiple_of(start, HALF_CHUNK), HALF_CHUNK), :],
                    sems.at[len(copies)],
                )
            )
    for copy in copies:
        copy.start()
    for copy in copies:
        copy.wait()

    one = lax.broadcasted_iota(jnp.int32, (TILE, TILE), 0)
    other = lax.broadcasted_iota(jnp.int32, (TILE, TILE), 1)
    identity = jnp.where(one == other, 1.0, 0.0).astype(jnp.bfloat16)

    def square_sum(tile):
        part = tile.astype(jnp.float32)
        return jnp.sum((part * part).reshape(TILE // 8, 8, TILE), axis=0)

    own = others = jnp.zeros((8, TILE), jnp.float32)
    for i in range(BLOCKS):
        for d in range(KEPT):
            j = (i + d) % BLOCKS
            for half in range(2):
                down = pl.ds(i * BLOCK + half * TILE, TILE)
                for column_half in range(2):
                    across = pl.ds(j * BLOCK + column_half * TILE, TILE)
                    tile = tiles[tile_rows(i, d, half, column_half), :]
                    gram[down, across] = tile
                    if d == 0:
                        own = own + square_sum(tile)
                    else:
                        others = others + square_sum(tile)
                        gram[across, down] = dot_nt(identity, tile).astype(jnp.bfloat16)
    quartic = jnp.full((1, 1), jnp.sum(own + 2.0 * others), jnp.float32)
    scale = 1.0 / jnp.sqrt(jnp.sqrt(quartic) + EPSILON)
    square = scale * scale

    state[...] = base_ref[...].astype(jnp.float32) * scale
    value[0] = state[...].astype(jnp.bfloat16)

    def step(number, _):
        now = lax.rem(number, 2)
        place = jnp.where(number < 2, number, lax.rem(number + 3, 5))
        cubic = (place == 0) | (place == 3)
        quintic = (place == 1) | (place == 4)
        keep = jnp.where(cubic, COEF_LINEAR, jnp.where(quintic, 1.0, 0.0))
        add = jnp.where(cubic, COEF_CUBIC, jnp.where(quintic, COEF_QUINTIC, 1.0))
        from_product = jnp.where(cubic, 1.0, 0.0)
        from_state = jnp.where(cubic, 0.0, 1.0)
        for strip in range(M // STRIP):
            cut = pl.ds(strip * STRIP, STRIP)
            product = square * jnp.dot(
                value[now], gram[:, cut], preferred_element_type=jnp.float32
            )
            result = keep * state[:, cut] + add * product
            state[:, cut] = result
            value[1 - now, :, cut] = (from_product * product + from_state * result).astype(
                jnp.bfloat16
            )

        @pl.when(number == 1)
        def _():
            total[...] = COEF_LINEAR * state[...]

        @pl.when(number == 6)
        def _():
            total[...] += COEF_CUBIC * state[...]

        return 0

    lax.fori_loop(0, STEPS, step, 0)
    update = (UPDATE_SCALE * (total[...] + COEF_QUINTIC * state[...])).astype(jnp.bfloat16)
    for r in range(ROWS):
        out_ref[r] = update[:, r * OWN_ROWS : (r + 1) * OWN_ROWS]


def newton_schulz(base, parts):
    return pl.pallas_call(
        newton_schulz_kernel,
        out_shape=jax.ShapeDtypeStruct((ROWS, OWN_COLS, OWN_ROWS), jnp.bfloat16),
        in_specs=[pl.BlockSpec(memory_space=pltpu.VMEM)]
        + [pl.BlockSpec(memory_space=pl.ANY)] * len(parts),
        out_specs=pl.BlockSpec(memory_space=pltpu.VMEM),
        scratch_shapes=[
            pltpu.VMEM((GRAM_ROWS, TILE), jnp.bfloat16),
            pltpu.VMEM((M, M), jnp.bfloat16),
            pltpu.VMEM((2, OWN_COLS, M), jnp.bfloat16),
            pltpu.VMEM((OWN_COLS, M), jnp.float32),
            pltpu.VMEM((OWN_COLS, M), jnp.float32),
            pltpu.SemaphoreType.DMA((sum(len(places) for places in PARTS),)),
        ],
        compiler_params=pltpu.CompilerParams(vmem_limit_bytes=58 * 2**20),
        name="newton_schulz",
    )(base, *parts)


def add_up(parts):
    total = parts[0].astype(jnp.float32)
    for part in parts[1:]:
        total = total + part.astype(jnp.float32)
    return total.astype(jnp.bfloat16)


def scattered_sum(chunks):
    received = [chunks[0]] + [over_x(chunks[k], k) for k in (2, 1, 3)]
    shares = over_z(add_up(received).reshape(Z_CHIPS, SHARE, TILE))
    return add_up([shares[z] for z in range(Z_CHIPS)])


def gathered(share):
    chunk = over_z(jnp.broadcast_to(share[None], (Z_CHIPS, SHARE, TILE))).reshape(CHUNK, TILE)
    first, second = chunk[:HALF_CHUNK], chunk[HALF_CHUNK:]
    from_x = {k: over_x(first, k) for k in (1, 3, 2)}
    from_y = {k: over_y(second, k) for k in (1, 3, 2)}
    first = jnp.stack([first] + [from_x[k] for k in (1, 2, 3)])
    second = jnp.stack([second] + [from_y[k] for k in (1, 2, 3)])
    first, second = lax.optimization_barrier((first, second))
    ups, downs = [over_y(first, 1), over_x(second, 1)], [over_y(first, 3), over_x(second, 3)]
    swapped = over_cores(jnp.concatenate([first, second]))
    onward = [up[:2] for up in ups], [down[2:] for down in downs]
    ups, downs, onward, swapped = lax.optimization_barrier((ups, downs, onward, swapped))
    far = []
    for over, up, down in zip((over_y, over_x), *onward):
        far += [over(up, 1), over(down, 3)]
    near = over_cores(jnp.concatenate(ups + downs))
    own_core = [first, second] + ups + downs + far
    return own_core + [swapped, near] + [over_cores(part) for part in far]


def per_device(gradient, momentum):
    grad32 = gradient.astype(jnp.float32)
    buffer = MOMENTUM_DECAY * momentum + grad32
    nesterov = grad32 + MOMENTUM_DECAY * buffer
    base = nesterov.astype(jnp.bfloat16)
    shifted = {k: over_y(base, k) for k in (1, 3, 2)}
    rows = [base] + [shifted[k] for k in (1, 2, 3)]
    chunks, columns = partial_gram(rows + [over_cores(part) for part in rows])
    parts = gathered(scattered_sum(chunks))
    update = newton_schulz(columns, parts)
    update = lax.all_to_all(update, "row", split_axis=0, concat_axis=0)
    update_matrix = update.reshape(PANEL_COLS, OWN_ROWS).T
    return (update_matrix, buffer)


def solution(mesh):
    return jax.shard_map(
        per_device,
        mesh=mesh,
        in_specs=(P("row", "col"), P("row", "col")),
        out_specs=(P("row", "col"), P("row", "col")),
        check_vma=False,
    )
```

```python
import math

import jax
import jax.numpy as jnp
from jax import lax
from jax.experimental import pallas as pl
from jax.experimental.pallas import tpu as pltpu
from jax.sharding import PartitionSpec as P

M = 3584
N = 12288
ROWS = 8
COLS = 32
X_CHIPS = 4
Y_CHIPS = 4
Z_CHIPS = 8
CORES = 2

MOMENTUM_DECAY = 0.95
EPSILON = 1e-07
COEF_LINEAR = 3.4445
COEF_CUBIC = -4.775
COEF_QUINTIC = 2.0315
UPDATE_SCALE = 0.2 * math.sqrt(max(M, N))

BLOCK = 512
BLOCKS = M // BLOCK
KEPT = (BLOCKS + 1) // 2
TILE = 256
TILES = BLOCKS * KEPT * 4
GRAM_ROWS = TILES * TILE
ROW_TILES = TILES // ROWS
PANEL_COLS = N // COLS
OWN_COLS = PANEL_COLS // ROWS
OWN_ROWS = M // ROWS
CHUNK = GRAM_ROWS // (ROWS * X_CHIPS)
SHARE = CHUNK // Z_CHIPS
HALF_CHUNK = CHUNK // 2
PIECE = TILE // 2
CHUNK_PIECES = CHUNK // PIECE
FIRST_PIECES = 5
FIRST_SHARE = FIRST_PIECES * PIECE // Z_CHIPS
OTHER_SHARE = SHARE - FIRST_SHARE
STEPS = 12
STRIP = M // 4

ALL_FOUR = (0, 1, 2, 3)


def line(half, last, others):
    return [(half, last, k) if half == 0 else (half, k, last) for k in others]


NEAR = [line(half, last, ALL_FOUR) for last in (0, 1, 3) for half in (0, 1)]
FAR = [line(half, 2, others) for half in (0, 1) for others in ((0, 1), (2, 3))]
OWN_PARTS = len(NEAR) + len(FAR)
PARTS = NEAR + FAR + [sum(NEAR[:2], []), sum(NEAR[2:], [])] + FAR

Z_GROUPS = [[x * Z_CHIPS + z for z in range(Z_CHIPS)] for x in range(X_CHIPS)]


def dot_nt(left, right):
    return lax.dot_general(
        left, right, (((1,), (1,)), ((), ())), preferred_element_type=jnp.float32
    )


def over_x(value, shift):
    pairs = [
        (x * Z_CHIPS + z, (x + shift) % X_CHIPS * Z_CHIPS + z)
        for x in range(X_CHIPS)
        for z in range(Z_CHIPS)
    ]
    return lax.ppermute(value, "col", pairs)


def over_y(value, shift):
    pairs = [
        (y * CORES + c, (y + shift) % Y_CHIPS * CORES + c)
        for y in range(Y_CHIPS)
        for c in range(CORES)
    ]
    return lax.ppermute(value, "row", pairs)


def over_cores(value):
    pairs = [
        (y * CORES + c, y * CORES + 1 - c) for y in range(Y_CHIPS) for c in range(CORES)
    ]
    return lax.ppermute(value, "row", pairs)


def over_z(value):
    return lax.all_to_all(
        value, "col", split_axis=0, concat_axis=0, axis_index_groups=Z_GROUPS
    )


def gram_kernel(*refs):
    row_refs, refs = refs[:ROWS], refs[ROWS:]
    chunk_refs, (others_ref, columns_ref, panel_ref, sems) = refs[:X_CHIPS], refs[X_CHIPS:]
    row = lax.axis_index("row")
    y, core = row // CORES, row % CORES
    copies = []
    for number, row_ref in enumerate(row_refs):
        shift, c = number % Y_CHIPS, core if number < Y_CHIPS else 1 - core
        owner = lax.rem(y + Y_CHIPS - shift, Y_CHIPS) * CORES + c
        copies.append(
            pltpu.make_async_copy(
                row_ref,
                panel_ref.at[pl.ds(pl.multiple_of(owner * OWN_ROWS, OWN_ROWS), OWN_ROWS), :],
                sems.at[number],
            )
        )
    for copy in copies:
        copy.start()
    for copy in copies:
        copy.wait()
    x = lax.axis_index("col") // Z_CHIPS
    wanted = row * OWN_COLS + lax.broadcasted_iota(jnp.int32, (OWN_COLS, PANEL_COLS), 0)
    column = lax.broadcasted_iota(jnp.int32, (OWN_COLS, PANEL_COLS), 1)
    pick = jnp.where(wanted == column, 1.0, 0.0).astype(jnp.bfloat16)
    for shift in range(X_CHIPS):
        owner = lax.rem(x + shift, X_CHIPS)
        for k in range(CHUNK_PIECES):
            piece = owner * CHUNK_PIECES + k
            tile = row * ROW_TILES + piece // 2
            block = tile // 4
            i, d = block // KEPT, block % KEPT
            j = lax.rem(i + d, BLOCKS)
            top = i * BLOCK + tile % 4 // 2 * TILE + piece % 2 * PIECE
            across = j * BLOCK + tile % 2 * TILE
            left = panel_ref[pl.ds(pl.multiple_of(top, PIECE), PIECE), :]
            right = panel_ref[pl.ds(pl.multiple_of(across, TILE), TILE), :]
            piece = dot_nt(left, right).astype(jnp.bfloat16)
            if k < FIRST_PIECES:
                chunk_refs[shift][k * PIECE : (k + 1) * PIECE, :] = piece
            else:
                for part in range(PIECE // OTHER_SHARE):
                    z = (k - FIRST_PIECES) * (PIECE // OTHER_SHARE) + part
                    others_ref[z, shift * OTHER_SHARE : (shift + 1) * OTHER_SHARE, :] = piece[
                        part * OTHER_SHARE : (part + 1) * OTHER_SHARE, :
                    ]
    for b in range(BLOCKS):
        rows = panel_ref[b * BLOCK : (b + 1) * BLOCK, :]
        columns_ref[:, b * BLOCK : (b + 1) * BLOCK] = dot_nt(pick, rows).astype(jnp.bfloat16)


def partial_gram(rows):
    vmem = pl.BlockSpec(memory_space=pltpu.VMEM)
    outs = pl.pallas_call(
        gram_kernel,
        out_shape=[jax.ShapeDtypeStruct((FIRST_PIECES * PIECE, TILE), jnp.bfloat16)] * X_CHIPS
        + [jax.ShapeDtypeStruct((Z_CHIPS, X_CHIPS * OTHER_SHARE, TILE), jnp.bfloat16)]
        + [jax.ShapeDtypeStruct((OWN_COLS, M), jnp.bfloat16)],
        in_specs=[pl.BlockSpec(memory_space=pl.ANY)] * ROWS,
        out_specs=[vmem] * (X_CHIPS + 2),
        scratch_shapes=[
            pltpu.VMEM((M, PANEL_COLS), jnp.bfloat16),
            pltpu.SemaphoreType.DMA((ROWS,)),
        ],
        compiler_params=pltpu.CompilerParams(vmem_limit_bytes=16 * 2**20),
        name="partial_gram",
    )(*rows)
    return outs[:X_CHIPS], outs[X_CHIPS], outs[X_CHIPS + 1]


def tile_rows(i, d, half, column_half):
    start = (((i * KEPT + d) * 2 + half) * 2 + column_half) * TILE
    return pl.ds(start, TILE)


def newton_schulz_kernel(base_ref, *refs):
    parts = refs[: len(PARTS)]
    out_ref, tiles, gram, value, state, total, sems = refs[len(PARTS) :]
    row = lax.axis_index("row")
    y, core = row // CORES, row % CORES
    x = lax.axis_index("col") // Z_CHIPS
    copies = []
    for number, (part, places) in enumerate(zip(parts, PARTS)):
        from_core = core if number < OWN_PARTS else 1 - core
        for k, (half, y_shift, x_shift) in enumerate(places):
            from_row = lax.rem(y + Y_CHIPS - y_shift, Y_CHIPS) * CORES + from_core
            from_x = lax.rem(x + X_CHIPS - x_shift, X_CHIPS)
            start = (from_row * X_CHIPS + from_x) * CHUNK + half * HALF_CHUNK
            copies.append(
                pltpu.make_async_copy(
                    part.at[k],
                    tiles.at[pl.ds(pl.multiple_of(start, HALF_CHUNK), HALF_CHUNK), :],
                    sems.at[len(copies)],
                )
            )
    for copy in copies:
        copy.start()
    for copy in copies:
        copy.wait()

    one = lax.broadcasted_iota(jnp.int32, (TILE, TILE), 0)
    other = lax.broadcasted_iota(jnp.int32, (TILE, TILE), 1)
    identity = jnp.where(one == other, 1.0, 0.0).astype(jnp.bfloat16)

    def square_sum(tile):
        part = tile.astype(jnp.float32)
        return jnp.sum((part * part).reshape(TILE // 8, 8, TILE), axis=0)

    own = others = jnp.zeros((8, TILE), jnp.float32)
    for i in range(BLOCKS):
        for d in range(KEPT):
            j = (i + d) % BLOCKS
            for half in range(2):
                down = pl.ds(i * BLOCK + half * TILE, TILE)
                for column_half in range(2):
                    across = pl.ds(j * BLOCK + column_half * TILE, TILE)
                    tile = tiles[tile_rows(i, d, half, column_half), :]
                    gram[down, across] = tile
                    if d == 0:
                        own = own + square_sum(tile)
                    else:
                        others = others + square_sum(tile)
                        gram[across, down] = dot_nt(identity, tile).astype(jnp.bfloat16)
    quartic = jnp.full((1, 1), jnp.sum(own + 2.0 * others), jnp.float32)
    scale = 1.0 / jnp.sqrt(jnp.sqrt(quartic) + EPSILON)
    square = scale * scale

    state[...] = base_ref[...].astype(jnp.float32) * scale
    value[0] = state[...].astype(jnp.bfloat16)

    def step(number, _):
        now = lax.rem(number, 2)
        place = jnp.where(number < 2, number, lax.rem(number + 3, 5))
        cubic = (place == 0) | (place == 3)
        quintic = (place == 1) | (place == 4)
        keep = jnp.where(cubic, COEF_LINEAR, jnp.where(quintic, 1.0, 0.0))
        add = jnp.where(cubic, COEF_CUBIC, jnp.where(quintic, COEF_QUINTIC, 1.0))
        from_product = jnp.where(cubic, 1.0, 0.0)
        from_state = jnp.where(cubic, 0.0, 1.0)
        for strip in range(M // STRIP):
            cut = pl.ds(strip * STRIP, STRIP)
            product = square * jnp.dot(
                value[now], gram[:, cut], preferred_element_type=jnp.float32
            )
            result = keep * state[:, cut] + add * product
            state[:, cut] = result
            value[1 - now, :, cut] = (from_product * product + from_state * result).astype(
                jnp.bfloat16
            )

        @pl.when(number == 1)
        def _():
            total[...] = COEF_LINEAR * state[...]

        @pl.when(number == 6)
        def _():
            total[...] += COEF_CUBIC * state[...]

        return 0

    lax.fori_loop(0, STEPS, step, 0)
    update = (UPDATE_SCALE * (total[...] + COEF_QUINTIC * state[...])).astype(jnp.bfloat16)
    for r in range(ROWS):
        out_ref[r] = update[:, r * OWN_ROWS : (r + 1) * OWN_ROWS]


def newton_schulz(base, parts):
    return pl.pallas_call(
        newton_schulz_kernel,
        out_shape=jax.ShapeDtypeStruct((ROWS, OWN_COLS, OWN_ROWS), jnp.bfloat16),
        in_specs=[pl.BlockSpec(memory_space=pltpu.VMEM)]
        + [pl.BlockSpec(memory_space=pl.ANY)] * len(parts),
        out_specs=pl.BlockSpec(memory_space=pltpu.VMEM),
        scratch_shapes=[
            pltpu.VMEM((GRAM_ROWS, TILE), jnp.bfloat16),
            pltpu.VMEM((M, M), jnp.bfloat16),
            pltpu.VMEM((2, OWN_COLS, M), jnp.bfloat16),
            pltpu.VMEM((OWN_COLS, M), jnp.float32),
            pltpu.VMEM((OWN_COLS, M), jnp.float32),
            pltpu.SemaphoreType.DMA((sum(len(places) for places in PARTS),)),
        ],
        compiler_params=pltpu.CompilerParams(vmem_limit_bytes=58 * 2**20),
        name="newton_schulz",
    )(base, *parts)


def add_up(parts):
    total = parts[0].astype(jnp.float32)
    for part in parts[1:]:
        total = total + part.astype(jnp.float32)
    return total.astype(jnp.bfloat16)


def scattered_sum(chunks, others):
    received = [chunks[0]] + [over_x(chunks[k], k) for k in (2, 1, 3)]
    others = over_z(others)
    others = add_up([others[z] for z in range(Z_CHIPS)]).reshape(X_CHIPS, OTHER_SHARE, TILE)
    others = [others[0]] + [over_x(others[k], k) for k in (2, 1, 3)]
    shares = over_z(add_up(received).reshape(Z_CHIPS, FIRST_SHARE, TILE))
    return jnp.concatenate([add_up([shares[z] for z in range(Z_CHIPS)]), add_up(others)])


def gathered(share):
    chunk = over_z(jnp.broadcast_to(share[None], (Z_CHIPS, SHARE, TILE)))
    chunk = [chunk[:, :FIRST_SHARE], chunk[:, FIRST_SHARE:]]
    chunk = jnp.concatenate([part.reshape(-1, TILE) for part in chunk])
    first, second = chunk[:HALF_CHUNK], chunk[HALF_CHUNK:]
    from_x = {k: over_x(first, k) for k in (1, 3, 2)}
    from_y = {k: over_y(second, k) for k in (1, 3, 2)}
    first = jnp.stack([first] + [from_x[k] for k in (1, 2, 3)])
    second = jnp.stack([second] + [from_y[k] for k in (1, 2, 3)])
    first, second = lax.optimization_barrier((first, second))
    ups, downs = [over_y(first, 1), over_x(second, 1)], [over_y(first, 3), over_x(second, 3)]
    swapped = over_cores(jnp.concatenate([first, second]))
    onward = [up[:2] for up in ups], [down[2:] for down in downs]
    ups, downs, onward, swapped = lax.optimization_barrier((ups, downs, onward, swapped))
    far = []
    for over, up, down in zip((over_y, over_x), *onward):
        far += [over(up, 1), over(down, 3)]
    near = over_cores(jnp.concatenate(ups + downs))
    own_core = [first, second] + ups + downs + far
    return own_core + [swapped, near] + [over_cores(part) for part in far]


def per_device(gradient, momentum):
    grad32 = gradient.astype(jnp.float32)
    buffer = MOMENTUM_DECAY * momentum + grad32
    nesterov = grad32 + MOMENTUM_DECAY * buffer
    base = nesterov.astype(jnp.bfloat16)
    shifted = {k: over_y(base, k) for k in (1, 3, 2)}
    rows = [base] + [shifted[k] for k in (1, 2, 3)]
    chunks, others, columns = partial_gram(rows + [over_cores(part) for part in rows])
    parts = gathered(scattered_sum(chunks, others))
    update = newton_schulz(columns, parts)
    update = lax.all_to_all(update, "row", split_axis=0, concat_axis=0)
    update_matrix = update.reshape(PANEL_COLS, OWN_ROWS).T
    return (update_matrix, buffer)


def solution(mesh):
    return jax.shard_map(
        per_device,
        mesh=mesh,
        in_specs=(P("row", "col"), P("row", "col")),
        out_specs=(P("row", "col"), P("row", "col")),
        check_vma=False,
    )
```

```python
import math

import jax
import jax.numpy as jnp
from jax import lax
from jax.experimental import pallas as pl
from jax.experimental.pallas import tpu as pltpu
from jax.sharding import PartitionSpec as P

M = 3584
N = 12288
ROWS = 8
COLS = 32
X_CHIPS = 4
Y_CHIPS = 4
Z_CHIPS = 8
CORES = 2

MOMENTUM_DECAY = 0.95
EPSILON = 1e-07
COEF_LINEAR = 3.4445
COEF_CUBIC = -4.775
COEF_QUINTIC = 2.0315
UPDATE_SCALE = 0.2 * math.sqrt(max(M, N))

BLOCK = 512
BLOCKS = M // BLOCK
KEPT = (BLOCKS + 1) // 2
TILE = 256
TILES = BLOCKS * KEPT * 4
GRAM_ROWS = TILES * TILE
ROW_TILES = TILES // ROWS
PANEL_COLS = N // COLS
OWN_COLS = PANEL_COLS // ROWS
OWN_ROWS = M // ROWS
CHUNK = GRAM_ROWS // (ROWS * X_CHIPS)
SHARE = CHUNK // Z_CHIPS
HALF_CHUNK = CHUNK // 2
PIECE = TILE // 2
CHUNK_PIECES = CHUNK // PIECE
FIRST_PIECES = 5
FIRST_SHARE = FIRST_PIECES * PIECE // Z_CHIPS
OTHER_SHARE = SHARE - FIRST_SHARE
STEPS = 12
STRIP = M // 4

ALL_FOUR = (0, 1, 2, 3)


def line(half, last, others):
    return [(half, last, k) if half == 0 else (half, k, last) for k in others]


NEAR = [line(half, last, ALL_FOUR) for last in (0, 1, 3) for half in (0, 1)]
FAR = [line(half, 2, others) for half in (0, 1) for others in ((0, 1), (2, 3))]
OWN_PARTS = len(NEAR) + len(FAR)
PARTS = NEAR + FAR + [sum(NEAR, [])] + FAR

Z_GROUPS = [[x * Z_CHIPS + z for z in range(Z_CHIPS)] for x in range(X_CHIPS)]


def dot_nt(left, right):
    return lax.dot_general(
        left, right, (((1,), (1,)), ((), ())), preferred_element_type=jnp.float32
    )


def over_x(value, shift):
    pairs = [
        (x * Z_CHIPS + z, (x + shift) % X_CHIPS * Z_CHIPS + z)
        for x in range(X_CHIPS)
        for z in range(Z_CHIPS)
    ]
    return lax.ppermute(value, "col", pairs)


def over_y(value, shift):
    pairs = [
        (y * CORES + c, (y + shift) % Y_CHIPS * CORES + c)
        for y in range(Y_CHIPS)
        for c in range(CORES)
    ]
    return lax.ppermute(value, "row", pairs)


def over_cores(value):
    pairs = [
        (y * CORES + c, y * CORES + 1 - c) for y in range(Y_CHIPS) for c in range(CORES)
    ]
    return lax.ppermute(value, "row", pairs)


def over_z(value):
    return lax.all_to_all(
        value, "col", split_axis=0, concat_axis=0, axis_index_groups=Z_GROUPS
    )


def gram_kernel(*refs):
    row_refs, refs = refs[:ROWS], refs[ROWS:]
    chunk_refs, (others_ref, columns_ref, panel_ref, sems) = refs[:X_CHIPS], refs[X_CHIPS:]
    row = lax.axis_index("row")
    y, core = row // CORES, row % CORES
    copies = []
    for number, row_ref in enumerate(row_refs):
        shift, c = number % Y_CHIPS, core if number < Y_CHIPS else 1 - core
        owner = lax.rem(y + Y_CHIPS - shift, Y_CHIPS) * CORES + c
        copies.append(
            pltpu.make_async_copy(
                row_ref,
                panel_ref.at[pl.ds(pl.multiple_of(owner * OWN_ROWS, OWN_ROWS), OWN_ROWS), :],
                sems.at[number],
            )
        )
    for copy in copies:
        copy.start()
    for copy in copies:
        copy.wait()
    x = lax.axis_index("col") // Z_CHIPS
    wanted = row * OWN_COLS + lax.broadcasted_iota(jnp.int32, (OWN_COLS, PANEL_COLS), 0)
    column = lax.broadcasted_iota(jnp.int32, (OWN_COLS, PANEL_COLS), 1)
    pick = jnp.where(wanted == column, 1.0, 0.0).astype(jnp.bfloat16)
    for shift in range(X_CHIPS):
        owner = lax.rem(x + shift, X_CHIPS)
        for k in range(CHUNK_PIECES):
            piece = owner * CHUNK_PIECES + k
            tile = row * ROW_TILES + piece // 2
            block = tile // 4
            i, d = block // KEPT, block % KEPT
            j = lax.rem(i + d, BLOCKS)
            top = i * BLOCK + tile % 4 // 2 * TILE + piece % 2 * PIECE
            across = j * BLOCK + tile % 2 * TILE
            left = panel_ref[pl.ds(pl.multiple_of(top, PIECE), PIECE), :]
            right = panel_ref[pl.ds(pl.multiple_of(across, TILE), TILE), :]
            piece = dot_nt(left, right).astype(jnp.bfloat16)
            if k < FIRST_PIECES:
                chunk_refs[shift][k * PIECE : (k + 1) * PIECE, :] = piece
            else:
                for part in range(PIECE // OTHER_SHARE):
                    z = (k - FIRST_PIECES) * (PIECE // OTHER_SHARE) + part
                    others_ref[z, shift * OTHER_SHARE : (shift + 1) * OTHER_SHARE, :] = piece[
                        part * OTHER_SHARE : (part + 1) * OTHER_SHARE, :
                    ]
    for b in range(BLOCKS):
        rows = panel_ref[b * BLOCK : (b + 1) * BLOCK, :]
        columns_ref[:, b * BLOCK : (b + 1) * BLOCK] = dot_nt(pick, rows).astype(jnp.bfloat16)


def partial_gram(rows):
    vmem = pl.BlockSpec(memory_space=pltpu.VMEM)
    outs = pl.pallas_call(
        gram_kernel,
        out_shape=[jax.ShapeDtypeStruct((FIRST_PIECES * PIECE, TILE), jnp.bfloat16)] * X_CHIPS
        + [jax.ShapeDtypeStruct((Z_CHIPS, X_CHIPS * OTHER_SHARE, TILE), jnp.bfloat16)]
        + [jax.ShapeDtypeStruct((OWN_COLS, M), jnp.bfloat16)],
        in_specs=[pl.BlockSpec(memory_space=pl.ANY)] * ROWS,
        out_specs=[vmem] * (X_CHIPS + 2),
        scratch_shapes=[
            pltpu.VMEM((M, PANEL_COLS), jnp.bfloat16),
            pltpu.SemaphoreType.DMA((ROWS,)),
        ],
        compiler_params=pltpu.CompilerParams(vmem_limit_bytes=16 * 2**20),
        name="partial_gram",
    )(*rows)
    return outs[:X_CHIPS], outs[X_CHIPS], outs[X_CHIPS + 1]


def tile_rows(i, d, half, column_half):
    start = (((i * KEPT + d) * 2 + half) * 2 + column_half) * TILE
    return pl.ds(start, TILE)


def newton_schulz_kernel(base_ref, *refs):
    parts = refs[: len(PARTS)]
    out_ref, tiles, gram, value, state, total, sems = refs[len(PARTS) :]
    row = lax.axis_index("row")
    y, core = row // CORES, row % CORES
    x = lax.axis_index("col") // Z_CHIPS
    copies = []
    for number, (part, places) in enumerate(zip(parts, PARTS)):
        from_core = core if number < OWN_PARTS else 1 - core
        for k, (half, y_shift, x_shift) in enumerate(places):
            from_row = lax.rem(y + Y_CHIPS - y_shift, Y_CHIPS) * CORES + from_core
            from_x = lax.rem(x + X_CHIPS - x_shift, X_CHIPS)
            start = (from_row * X_CHIPS + from_x) * CHUNK + half * HALF_CHUNK
            copies.append(
                pltpu.make_async_copy(
                    part.at[k],
                    tiles.at[pl.ds(pl.multiple_of(start, HALF_CHUNK), HALF_CHUNK), :],
                    sems.at[len(copies)],
                )
            )
    for copy in copies:
        copy.start()
    for copy in copies:
        copy.wait()

    one = lax.broadcasted_iota(jnp.int32, (TILE, TILE), 0)
    other = lax.broadcasted_iota(jnp.int32, (TILE, TILE), 1)
    identity = jnp.where(one == other, 1.0, 0.0).astype(jnp.bfloat16)

    def square_sum(tile):
        part = tile.astype(jnp.float32)
        return jnp.sum((part * part).reshape(TILE // 8, 8, TILE), axis=0)

    own = others = jnp.zeros((8, TILE), jnp.float32)
    for i in range(BLOCKS):
        for d in range(KEPT):
            j = (i + d) % BLOCKS
            for half in range(2):
                down = pl.ds(i * BLOCK + half * TILE, TILE)
                for column_half in range(2):
                    across = pl.ds(j * BLOCK + column_half * TILE, TILE)
                    tile = tiles[tile_rows(i, d, half, column_half), :]
                    gram[down, across] = tile
                    if d == 0:
                        own = own + square_sum(tile)
                    else:
                        others = others + square_sum(tile)
                        gram[across, down] = dot_nt(identity, tile).astype(jnp.bfloat16)
    quartic = jnp.full((1, 1), jnp.sum(own + 2.0 * others), jnp.float32)
    scale = 1.0 / jnp.sqrt(jnp.sqrt(quartic) + EPSILON)
    square = scale * scale

    state[...] = base_ref[...].astype(jnp.float32) * scale
    value[0] = state[...].astype(jnp.bfloat16)

    def step(number, _):
        now = lax.rem(number, 2)
        place = jnp.where(number < 2, number, lax.rem(number + 3, 5))
        cubic = (place == 0) | (place == 3)
        quintic = (place == 1) | (place == 4)
        keep = jnp.where(cubic, COEF_LINEAR, jnp.where(quintic, 1.0, 0.0))
        add = jnp.where(cubic, COEF_CUBIC, jnp.where(quintic, COEF_QUINTIC, 1.0))
        from_product = jnp.where(cubic, 1.0, 0.0)
        from_state = jnp.where(cubic, 0.0, 1.0)
        for strip in range(M // STRIP):
            cut = pl.ds(strip * STRIP, STRIP)
            upper = jnp.dot(
                value[now, :, : M // 2], gram[: M // 2, cut], preferred_element_type=jnp.float32
            )
            lower = jnp.dot(
                value[now, :, M // 2 :], gram[M // 2 :, cut], preferred_element_type=jnp.float32
            )
            product = square * (upper + lower)
            result = keep * state[:, cut] + add * product
            state[:, cut] = result
            value[1 - now, :, cut] = (from_product * product + from_state * result).astype(
                jnp.bfloat16
            )

        @pl.when(number == 1)
        def _():
            total[...] = COEF_LINEAR * state[...]

        @pl.when(number == 6)
        def _():
            total[...] += COEF_CUBIC * state[...]

        return 0

    lax.fori_loop(0, STEPS, step, 0)
    update = (UPDATE_SCALE * (total[...] + COEF_QUINTIC * state[...])).astype(jnp.bfloat16)
    for r in range(ROWS):
        out_ref[r] = update[:, r * OWN_ROWS : (r + 1) * OWN_ROWS]


def newton_schulz(base, parts):
    return pl.pallas_call(
        newton_schulz_kernel,
        out_shape=jax.ShapeDtypeStruct((ROWS, OWN_COLS, OWN_ROWS), jnp.bfloat16),
        in_specs=[pl.BlockSpec(memory_space=pltpu.VMEM)]
        + [pl.BlockSpec(memory_space=pl.ANY)] * len(parts),
        out_specs=pl.BlockSpec(memory_space=pltpu.VMEM),
        scratch_shapes=[
            pltpu.VMEM((GRAM_ROWS, TILE), jnp.bfloat16),
            pltpu.VMEM((M, M), jnp.bfloat16),
            pltpu.VMEM((2, OWN_COLS, M), jnp.bfloat16),
            pltpu.VMEM((OWN_COLS, M), jnp.float32),
            pltpu.VMEM((OWN_COLS, M), jnp.float32),
            pltpu.SemaphoreType.DMA((sum(len(places) for places in PARTS),)),
        ],
        compiler_params=pltpu.CompilerParams(vmem_limit_bytes=58 * 2**20),
        name="newton_schulz",
    )(base, *parts)


def add_up(parts):
    total = parts[0].astype(jnp.float32)
    for part in parts[1:]:
        total = total + part.astype(jnp.float32)
    return total.astype(jnp.bfloat16)


def scattered_sum(chunks, others):
    received = [chunks[0]] + [over_x(chunks[k], k) for k in (2, 1, 3)]
    others = over_z(others)
    others = add_up([others[z] for z in range(Z_CHIPS)]).reshape(X_CHIPS, OTHER_SHARE, TILE)
    others = [others[0]] + [over_x(others[k], k) for k in (2, 1, 3)]
    shares = over_z(add_up(received).reshape(Z_CHIPS, FIRST_SHARE, TILE))
    return jnp.concatenate([add_up([shares[z] for z in range(Z_CHIPS)]), add_up(others)])


def gathered(share):
    chunk = over_z(jnp.broadcast_to(share[None], (Z_CHIPS, SHARE, TILE)))
    chunk = [chunk[:, :FIRST_SHARE], chunk[:, FIRST_SHARE:]]
    chunk = jnp.concatenate([part.reshape(-1, TILE) for part in chunk])
    first, second = chunk[:HALF_CHUNK], chunk[HALF_CHUNK:]
    from_x = {k: over_x(first, k) for k in (1, 3, 2)}
    from_y = {k: over_y(second, k) for k in (1, 3, 2)}
    first = jnp.stack([first] + [from_x[k] for k in (1, 2, 3)])
    second = jnp.stack([second] + [from_y[k] for k in (1, 2, 3)])
    first, second = lax.optimization_barrier((first, second))
    ups, downs = [over_y(first, 1), over_x(second, 1)], [over_y(first, 3), over_x(second, 3)]
    onward = [up[:2] for up in ups], [down[2:] for down in downs]
    ups, downs, onward = lax.optimization_barrier((ups, downs, onward))
    far = []
    for over, up, down in zip((over_y, over_x), *onward):
        far += [over(up, 1), over(down, 3)]
    near = over_cores(jnp.concatenate([first, second] + ups + downs))
    sent, near = lax.optimization_barrier((far, near))
    own_core = [first, second] + ups + downs + far
    return own_core + [near] + [over_cores(part) for part in sent]


def per_device(gradient, momentum):
    grad32 = gradient.astype(jnp.float32)
    buffer = MOMENTUM_DECAY * momentum + grad32
    nesterov = grad32 + MOMENTUM_DECAY * buffer
    base = nesterov.astype(jnp.bfloat16)
    shifted = {k: over_y(base, k) for k in (1, 3, 2)}
    rows = [base] + [shifted[k] for k in (1, 2, 3)]
    chunks, others, columns = partial_gram(rows + [over_cores(part) for part in rows])
    parts = gathered(scattered_sum(chunks, others))
    update = newton_schulz(columns, parts)
    update = lax.all_to_all(update, "row", split_axis=0, concat_axis=0)
    update_matrix = update.reshape(PANEL_COLS, OWN_ROWS).T
    return (update_matrix, buffer)


def solution(mesh):
    return jax.shard_map(
        per_device,
        mesh=mesh,
        in_specs=(P("row", "col"), P("row", "col")),
        out_specs=(P("row", "col"), P("row", "col")),
        check_vma=False,
    )
```

```python
import math

import jax
import jax.numpy as jnp
from jax import lax
from jax.experimental import pallas as pl
from jax.experimental.pallas import tpu as pltpu
from jax.sharding import PartitionSpec as P

M = 3584
N = 12288
ROWS = 8
COLS = 32
X_CHIPS = 4
Y_CHIPS = 4
Z_CHIPS = 8
CORES = 2

MOMENTUM_DECAY = 0.95
EPSILON = 1e-07
COEF_LINEAR = 3.4445
COEF_CUBIC = -4.775
COEF_QUINTIC = 2.0315
UPDATE_SCALE = 0.2 * math.sqrt(max(M, N))

BLOCK = 512
BLOCKS = M // BLOCK
KEPT = (BLOCKS + 1) // 2
TILE = 256
TILES = BLOCKS * KEPT * 4
GRAM_ROWS = TILES * TILE
ROW_TILES = TILES // ROWS
PANEL_COLS = N // COLS
OWN_COLS = PANEL_COLS // ROWS
OWN_ROWS = M // ROWS
CHUNK = GRAM_ROWS // (ROWS * X_CHIPS)
SHARE = CHUNK // Z_CHIPS
HALF_CHUNK = CHUNK // 2
PIECE = TILE // 2
CHUNK_PIECES = CHUNK // PIECE
FIRST_PIECES = 4
FIRST_SHARE = FIRST_PIECES * PIECE // Z_CHIPS
OTHER_SHARE = SHARE - FIRST_SHARE
STEPS = 12
STRIP = M // 4

ALL_FOUR = (0, 1, 2, 3)


def line(half, last, others):
    return [(half, last, k) if half == 0 else (half, k, last) for k in others]


NEAR = [line(half, last, ALL_FOUR) for last in (0, 1, 3) for half in (0, 1)]
FAR = [line(half, 2, others) for half in (0, 1) for others in ((0, 1), (2, 3))]
OWN_PARTS = len(NEAR) + len(FAR)
PARTS = NEAR + FAR + [sum(NEAR, [])] + FAR

Z_GROUPS = [[x * Z_CHIPS + z for z in range(Z_CHIPS)] for x in range(X_CHIPS)]


def dot_nt(left, right):
    return lax.dot_general(
        left, right, (((1,), (1,)), ((), ())), preferred_element_type=jnp.float32
    )


def over_x(value, shift):
    pairs = [
        (x * Z_CHIPS + z, (x + shift) % X_CHIPS * Z_CHIPS + z)
        for x in range(X_CHIPS)
        for z in range(Z_CHIPS)
    ]
    return lax.ppermute(value, "col", pairs)


def over_y(value, shift):
    pairs = [
        (y * CORES + c, (y + shift) % Y_CHIPS * CORES + c)
        for y in range(Y_CHIPS)
        for c in range(CORES)
    ]
    return lax.ppermute(value, "row", pairs)


def over_cores(value):
    pairs = [
        (y * CORES + c, y * CORES + 1 - c) for y in range(Y_CHIPS) for c in range(CORES)
    ]
    return lax.ppermute(value, "row", pairs)


def over_z(value):
    return lax.all_to_all(
        value, "col", split_axis=0, concat_axis=0, axis_index_groups=Z_GROUPS
    )


def gram_kernel(*refs):
    row_refs, refs = refs[:ROWS], refs[ROWS:]
    chunk_refs, (others_ref, columns_ref, panel_ref, sems) = refs[:X_CHIPS], refs[X_CHIPS:]
    row = lax.axis_index("row")
    y, core = row // CORES, row % CORES
    copies = []
    for number, row_ref in enumerate(row_refs):
        shift, c = number % Y_CHIPS, core if number < Y_CHIPS else 1 - core
        owner = lax.rem(y + Y_CHIPS - shift, Y_CHIPS) * CORES + c
        copies.append(
            pltpu.make_async_copy(
                row_ref,
                panel_ref.at[pl.ds(pl.multiple_of(owner * OWN_ROWS, OWN_ROWS), OWN_ROWS), :],
                sems.at[number],
            )
        )
    for copy in copies:
        copy.start()
    for copy in copies:
        copy.wait()
    x = lax.axis_index("col") // Z_CHIPS
    wanted = row * OWN_COLS + lax.broadcasted_iota(jnp.int32, (OWN_COLS, PANEL_COLS), 0)
    column = lax.broadcasted_iota(jnp.int32, (OWN_COLS, PANEL_COLS), 1)
    pick = jnp.where(wanted == column, 1.0, 0.0).astype(jnp.bfloat16)
    for shift in range(X_CHIPS):
        owner = lax.rem(x + shift, X_CHIPS)
        rest = []
        for k in range(CHUNK_PIECES):
            piece = owner * CHUNK_PIECES + k
            tile = row * ROW_TILES + piece // 2
            block = tile // 4
            i, d = block // KEPT, block % KEPT
            j = lax.rem(i + d, BLOCKS)
            top = i * BLOCK + tile % 4 // 2 * TILE + piece % 2 * PIECE
            across = j * BLOCK + tile % 2 * TILE
            left = panel_ref[pl.ds(pl.multiple_of(top, PIECE), PIECE), :]
            right = panel_ref[pl.ds(pl.multiple_of(across, TILE), TILE), :]
            piece = dot_nt(left, right).astype(jnp.bfloat16)
            if k < FIRST_PIECES:
                chunk_refs[shift][k * PIECE : (k + 1) * PIECE, :] = piece
            else:
                rest.append(piece)
        rest = jnp.concatenate(rest)
        for z in range(Z_CHIPS):
            others_ref[z, shift * OTHER_SHARE : (shift + 1) * OTHER_SHARE, :] = rest[
                z * OTHER_SHARE : (z + 1) * OTHER_SHARE, :
            ]
    for b in range(BLOCKS):
        rows = panel_ref[b * BLOCK : (b + 1) * BLOCK, :]
        columns_ref[:, b * BLOCK : (b + 1) * BLOCK] = dot_nt(pick, rows).astype(jnp.bfloat16)


def partial_gram(rows):
    vmem = pl.BlockSpec(memory_space=pltpu.VMEM)
    outs = pl.pallas_call(
        gram_kernel,
        out_shape=[jax.ShapeDtypeStruct((FIRST_PIECES * PIECE, TILE), jnp.bfloat16)] * X_CHIPS
        + [jax.ShapeDtypeStruct((Z_CHIPS, X_CHIPS * OTHER_SHARE, TILE), jnp.bfloat16)]
        + [jax.ShapeDtypeStruct((OWN_COLS, M), jnp.bfloat16)],
        in_specs=[pl.BlockSpec(memory_space=pl.ANY)] * ROWS,
        out_specs=[vmem] * (X_CHIPS + 2),
        scratch_shapes=[
            pltpu.VMEM((M, PANEL_COLS), jnp.bfloat16),
            pltpu.SemaphoreType.DMA((ROWS,)),
        ],
        compiler_params=pltpu.CompilerParams(vmem_limit_bytes=16 * 2**20),
        name="partial_gram",
    )(*rows)
    return outs[:X_CHIPS], outs[X_CHIPS], outs[X_CHIPS + 1]


def tile_rows(i, d, half, column_half):
    start = (((i * KEPT + d) * 2 + half) * 2 + column_half) * TILE
    return pl.ds(start, TILE)


def newton_schulz_kernel(base_ref, *refs):
    parts = refs[: len(PARTS)]
    out_ref, tiles, gram, value, state, total, sems = refs[len(PARTS) :]
    row = lax.axis_index("row")
    y, core = row // CORES, row % CORES
    x = lax.axis_index("col") // Z_CHIPS
    copies = []
    for number, (part, places) in enumerate(zip(parts, PARTS)):
        from_core = core if number < OWN_PARTS else 1 - core
        for k, (half, y_shift, x_shift) in enumerate(places):
            from_row = lax.rem(y + Y_CHIPS - y_shift, Y_CHIPS) * CORES + from_core
            from_x = lax.rem(x + X_CHIPS - x_shift, X_CHIPS)
            start = (from_row * X_CHIPS + from_x) * CHUNK + half * HALF_CHUNK
            copies.append(
                pltpu.make_async_copy(
                    part.at[k],
                    tiles.at[pl.ds(pl.multiple_of(start, HALF_CHUNK), HALF_CHUNK), :],
                    sems.at[len(copies)],
                )
            )
    for copy in copies:
        copy.start()
    for copy in copies:
        copy.wait()

    one = lax.broadcasted_iota(jnp.int32, (TILE, TILE), 0)
    other = lax.broadcasted_iota(jnp.int32, (TILE, TILE), 1)
    identity = jnp.where(one == other, 1.0, 0.0).astype(jnp.bfloat16)

    def square_sum(tile):
        part = tile.astype(jnp.float32)
        return jnp.sum((part * part).reshape(TILE // 8, 8, TILE), axis=0)

    own = others = jnp.zeros((8, TILE), jnp.float32)
    for i in range(BLOCKS):
        for d in range(KEPT):
            j = (i + d) % BLOCKS
            for half in range(2):
                down = pl.ds(i * BLOCK + half * TILE, TILE)
                for column_half in range(2):
                    across = pl.ds(j * BLOCK + column_half * TILE, TILE)
                    tile = tiles[tile_rows(i, d, half, column_half), :]
                    gram[down, across] = tile
                    if d == 0:
                        own = own + square_sum(tile)
                    else:
                        others = others + square_sum(tile)
                        gram[across, down] = dot_nt(identity, tile).astype(jnp.bfloat16)
    quartic = jnp.full((1, 1), jnp.sum(own + 2.0 * others), jnp.float32)
    scale = 1.0 / jnp.sqrt(jnp.sqrt(quartic) + EPSILON)
    square = scale * scale

    state[...] = base_ref[...].astype(jnp.float32) * scale
    value[0] = state[...].astype(jnp.bfloat16)

    def step(number, _):
        now = lax.rem(number, 2)
        place = jnp.where(number < 2, number, lax.rem(number + 3, 5))
        cubic = (place == 0) | (place == 3)
        quintic = (place == 1) | (place == 4)
        keep = jnp.where(cubic, COEF_LINEAR, jnp.where(quintic, 1.0, 0.0))
        add = jnp.where(cubic, COEF_CUBIC, jnp.where(quintic, COEF_QUINTIC, 1.0))
        from_product = jnp.where(cubic, 1.0, 0.0)
        from_state = jnp.where(cubic, 0.0, 1.0)
        for strip in range(M // STRIP):
            cut = pl.ds(strip * STRIP, STRIP)
            upper = jnp.dot(
                value[now, :, : M // 2], gram[: M // 2, cut], preferred_element_type=jnp.float32
            )
            lower = jnp.dot(
                value[now, :, M // 2 :], gram[M // 2 :, cut], preferred_element_type=jnp.float32
            )
            product = square * (upper + lower)
            result = keep * state[:, cut] + add * product
            state[:, cut] = result
            value[1 - now, :, cut] = (from_product * product + from_state * result).astype(
                jnp.bfloat16
            )

        @pl.when(number == 1)
        def _():
            total[...] = COEF_LINEAR * state[...]

        @pl.when(number == 6)
        def _():
            total[...] += COEF_CUBIC * state[...]

        return 0

    lax.fori_loop(0, STEPS, step, 0)
    update = (UPDATE_SCALE * (total[...] + COEF_QUINTIC * state[...])).astype(jnp.bfloat16)
    for r in range(ROWS):
        out_ref[r] = update[:, r * OWN_ROWS : (r + 1) * OWN_ROWS]


def newton_schulz(base, parts):
    return pl.pallas_call(
        newton_schulz_kernel,
        out_shape=jax.ShapeDtypeStruct((ROWS, OWN_COLS, OWN_ROWS), jnp.bfloat16),
        in_specs=[pl.BlockSpec(memory_space=pltpu.VMEM)]
        + [pl.BlockSpec(memory_space=pl.ANY)] * len(parts),
        out_specs=pl.BlockSpec(memory_space=pltpu.VMEM),
        scratch_shapes=[
            pltpu.VMEM((GRAM_ROWS, TILE), jnp.bfloat16),
            pltpu.VMEM((M, M), jnp.bfloat16),
            pltpu.VMEM((2, OWN_COLS, M), jnp.bfloat16),
            pltpu.VMEM((OWN_COLS, M), jnp.float32),
            pltpu.VMEM((OWN_COLS, M), jnp.float32),
            pltpu.SemaphoreType.DMA((sum(len(places) for places in PARTS),)),
        ],
        compiler_params=pltpu.CompilerParams(vmem_limit_bytes=58 * 2**20),
        name="newton_schulz",
    )(base, *parts)


def add_up(parts):
    total = parts[0].astype(jnp.float32)
    for part in parts[1:]:
        total = total + part.astype(jnp.float32)
    return total.astype(jnp.bfloat16)


def scattered_sum(chunks, others):
    received = [chunks[0]] + [over_x(chunks[k], k) for k in (2, 1, 3)]
    others = over_z(others)
    others = add_up([others[z] for z in range(Z_CHIPS)]).reshape(X_CHIPS, OTHER_SHARE, TILE)
    others = [others[0]] + [over_x(others[k], k) for k in (2, 1, 3)]
    shares = over_z(add_up(received).reshape(Z_CHIPS, FIRST_SHARE, TILE))
    return jnp.concatenate([add_up([shares[z] for z in range(Z_CHIPS)]), add_up(others)])


def gathered(share):
    chunk = over_z(jnp.broadcast_to(share[None], (Z_CHIPS, SHARE, TILE)))
    chunk = [chunk[:, :FIRST_SHARE], chunk[:, FIRST_SHARE:]]
    chunk = jnp.concatenate([part.reshape(-1, TILE) for part in chunk])
    first, second = chunk[:HALF_CHUNK], chunk[HALF_CHUNK:]
    from_x = {k: over_x(first, k) for k in (1, 3, 2)}
    from_y = {k: over_y(second, k) for k in (1, 3, 2)}
    first = jnp.stack([first] + [from_x[k] for k in (1, 2, 3)])
    second = jnp.stack([second] + [from_y[k] for k in (1, 2, 3)])
    first, second = lax.optimization_barrier((first, second))
    ups, downs = [over_y(first, 1), over_x(second, 1)], [over_y(first, 3), over_x(second, 3)]
    onward = [up[:2] for up in ups], [down[2:] for down in downs]
    ups, downs, onward = lax.optimization_barrier((ups, downs, onward))
    far = []
    for over, up, down in zip((over_y, over_x), *onward):
        far += [over(up, 1), over(down, 3)]
    near = over_cores(jnp.concatenate([first, second] + ups + downs))
    sent, near = lax.optimization_barrier((far, near))
    own_core = [first, second] + ups + downs + far
    return own_core + [near] + [over_cores(part) for part in sent]


def per_device(gradient, momentum):
    grad32 = gradient.astype(jnp.float32)
    buffer = MOMENTUM_DECAY * momentum + grad32
    nesterov = grad32 + MOMENTUM_DECAY * buffer
    base = nesterov.astype(jnp.bfloat16)
    shifted = {k: over_y(base, k) for k in (1, 3, 2)}
    rows = [base] + [shifted[k] for k in (1, 2, 3)]
    chunks, others, columns = partial_gram(rows + [over_cores(part) for part in rows])
    parts = gathered(scattered_sum(chunks, others))
    update = newton_schulz(columns, parts)
    update = lax.all_to_all(update, "row", split_axis=0, concat_axis=0)
    update_matrix = update.reshape(PANEL_COLS, OWN_ROWS).T
    return (update_matrix, buffer)


def solution(mesh):
    return jax.shard_map(
        per_device,
        mesh=mesh,
        in_specs=(P("row", "col"), P("row", "col")),
        out_specs=(P("row", "col"), P("row", "col")),
        check_vma=False,
    )
```

```python
import math

import jax
import jax.numpy as jnp
from jax import lax
from jax.experimental import pallas as pl
from jax.experimental.pallas import tpu as pltpu
from jax.sharding import PartitionSpec as P

M = 3584
N = 12288
ROWS = 8
COLS = 32
X_CHIPS = 4
Y_CHIPS = 4
Z_CHIPS = 8
CORES = 2

MOMENTUM_DECAY = 0.95
EPSILON = 1e-07
COEF_LINEAR = 3.4445
COEF_CUBIC = -4.775
COEF_QUINTIC = 2.0315
UPDATE_SCALE = 0.2 * math.sqrt(max(M, N))

BLOCK = 512
BLOCKS = M // BLOCK
KEPT = (BLOCKS + 1) // 2
TILE = 256
TILES = BLOCKS * KEPT * 4
GRAM_ROWS = TILES * TILE
ROW_TILES = TILES // ROWS
PANEL_COLS = N // COLS
OWN_COLS = PANEL_COLS // ROWS
OWN_ROWS = M // ROWS
CHUNK = GRAM_ROWS // (ROWS * X_CHIPS)
SHARE = CHUNK // Z_CHIPS
HALF_CHUNK = CHUNK // 2
PIECE = TILE // 2
CHUNK_PIECES = CHUNK // PIECE
FIRST_PIECES = 4
FIRST_SHARE = FIRST_PIECES * PIECE // Z_CHIPS
OTHER_SHARE = SHARE - FIRST_SHARE
STEPS = 12
STRIP = M // 4

ALL_FOUR = (0, 1, 2, 3)


def line(half, last, others):
    return [(half, last, k) if half == 0 else (half, k, last) for k in others]


NEAR = [line(half, last, ALL_FOUR) for last in (0, 1, 3) for half in (0, 1)]
FAR = [line(half, 2, others) for half in (0, 1) for others in ((0, 1), (2, 3))]
OWN_PARTS = len(NEAR) + len(FAR)
PARTS = NEAR + FAR + [sum(NEAR, []), sum(FAR, [])]

Z_GROUPS = [[x * Z_CHIPS + z for z in range(Z_CHIPS)] for x in range(X_CHIPS)]


def dot_nt(left, right):
    return lax.dot_general(
        left, right, (((1,), (1,)), ((), ())), preferred_element_type=jnp.float32
    )


def over_x(value, shift):
    pairs = [
        (x * Z_CHIPS + z, (x + shift) % X_CHIPS * Z_CHIPS + z)
        for x in range(X_CHIPS)
        for z in range(Z_CHIPS)
    ]
    return lax.ppermute(value, "col", pairs)


def over_y(value, shift):
    pairs = [
        (y * CORES + c, (y + shift) % Y_CHIPS * CORES + c)
        for y in range(Y_CHIPS)
        for c in range(CORES)
    ]
    return lax.ppermute(value, "row", pairs)


def over_cores(value):
    pairs = [
        (y * CORES + c, y * CORES + 1 - c) for y in range(Y_CHIPS) for c in range(CORES)
    ]
    return lax.ppermute(value, "row", pairs)


def over_z(value):
    return lax.all_to_all(
        value, "col", split_axis=0, concat_axis=0, axis_index_groups=Z_GROUPS
    )


def gram_kernel(*refs):
    row_refs, refs = refs[:ROWS], refs[ROWS:]
    chunk_refs, (others_ref, columns_ref, panel_ref, sems) = refs[:X_CHIPS], refs[X_CHIPS:]
    row = lax.axis_index("row")
    y, core = row // CORES, row % CORES
    copies = []
    for number, row_ref in enumerate(row_refs):
        shift, c = number % Y_CHIPS, core if number < Y_CHIPS else 1 - core
        owner = lax.rem(y + Y_CHIPS - shift, Y_CHIPS) * CORES + c
        copies.append(
            pltpu.make_async_copy(
                row_ref,
                panel_ref.at[pl.ds(pl.multiple_of(owner * OWN_ROWS, OWN_ROWS), OWN_ROWS), :],
                sems.at[number],
            )
        )
    for copy in copies:
        copy.start()
    for copy in copies:
        copy.wait()
    x = lax.axis_index("col") // Z_CHIPS
    wanted = row * OWN_COLS + lax.broadcasted_iota(jnp.int32, (OWN_COLS, PANEL_COLS), 0)
    column = lax.broadcasted_iota(jnp.int32, (OWN_COLS, PANEL_COLS), 1)
    pick = jnp.where(wanted == column, 1.0, 0.0).astype(jnp.bfloat16)
    for shift in range(X_CHIPS):
        owner = lax.rem(x + shift, X_CHIPS)
        rest = []
        for k in range(CHUNK_PIECES):
            piece = owner * CHUNK_PIECES + k
            tile = row * ROW_TILES + piece // 2
            block = tile // 4
            i, d = block // KEPT, block % KEPT
            j = lax.rem(i + d, BLOCKS)
            top = i * BLOCK + tile % 4 // 2 * TILE + piece % 2 * PIECE
            across = j * BLOCK + tile % 2 * TILE
            left = panel_ref[pl.ds(pl.multiple_of(top, PIECE), PIECE), :]
            right = panel_ref[pl.ds(pl.multiple_of(across, TILE), TILE), :]
            piece = dot_nt(left, right).astype(jnp.bfloat16)
            if k < FIRST_PIECES:
                chunk_refs[shift][k * PIECE : (k + 1) * PIECE, :] = piece
            else:
                rest.append(piece)
        rest = jnp.concatenate(rest)
        for z in range(Z_CHIPS):
            others_ref[z, shift * OTHER_SHARE : (shift + 1) * OTHER_SHARE, :] = rest[
                z * OTHER_SHARE : (z + 1) * OTHER_SHARE, :
            ]
    for b in range(BLOCKS):
        rows = panel_ref[b * BLOCK : (b + 1) * BLOCK, :]
        columns_ref[:, b * BLOCK : (b + 1) * BLOCK] = dot_nt(pick, rows).astype(jnp.bfloat16)


def partial_gram(rows):
    vmem = pl.BlockSpec(memory_space=pltpu.VMEM)
    outs = pl.pallas_call(
        gram_kernel,
        out_shape=[jax.ShapeDtypeStruct((FIRST_PIECES * PIECE, TILE), jnp.bfloat16)] * X_CHIPS
        + [jax.ShapeDtypeStruct((Z_CHIPS, X_CHIPS * OTHER_SHARE, TILE), jnp.bfloat16)]
        + [jax.ShapeDtypeStruct((OWN_COLS, M), jnp.bfloat16)],
        in_specs=[pl.BlockSpec(memory_space=pl.ANY)] * ROWS,
        out_specs=[vmem] * (X_CHIPS + 2),
        scratch_shapes=[
            pltpu.VMEM((M, PANEL_COLS), jnp.bfloat16),
            pltpu.SemaphoreType.DMA((ROWS,)),
        ],
        compiler_params=pltpu.CompilerParams(vmem_limit_bytes=16 * 2**20),
        name="partial_gram",
    )(*rows)
    return outs[:X_CHIPS], outs[X_CHIPS], outs[X_CHIPS + 1]


def tile_rows(i, d, half, column_half):
    start = (((i * KEPT + d) * 2 + half) * 2 + column_half) * TILE
    return pl.ds(start, TILE)


def newton_schulz_kernel(base_ref, *refs):
    parts = refs[: len(PARTS)]
    out_ref, tiles, gram, value, state, total, sems = refs[len(PARTS) :]
    row = lax.axis_index("row")
    y, core = row // CORES, row % CORES
    x = lax.axis_index("col") // Z_CHIPS
    copies = []
    for number, (part, places) in enumerate(zip(parts, PARTS)):
        from_core = core if number < OWN_PARTS else 1 - core
        for k, (half, y_shift, x_shift) in enumerate(places):
            from_row = lax.rem(y + Y_CHIPS - y_shift, Y_CHIPS) * CORES + from_core
            from_x = lax.rem(x + X_CHIPS - x_shift, X_CHIPS)
            start = (from_row * X_CHIPS + from_x) * CHUNK + half * HALF_CHUNK
            copies.append(
                pltpu.make_async_copy(
                    part.at[k],
                    tiles.at[pl.ds(pl.multiple_of(start, HALF_CHUNK), HALF_CHUNK), :],
                    sems.at[len(copies)],
                )
            )
    for copy in copies:
        copy.start()
    for copy in copies:
        copy.wait()

    one = lax.broadcasted_iota(jnp.int32, (TILE, TILE), 0)
    other = lax.broadcasted_iota(jnp.int32, (TILE, TILE), 1)
    identity = jnp.where(one == other, 1.0, 0.0).astype(jnp.bfloat16)

    def square_sum(tile):
        part = tile.astype(jnp.float32)
        return jnp.sum((part * part).reshape(TILE // 8, 8, TILE), axis=0)

    own = others = jnp.zeros((8, TILE), jnp.float32)
    for i in range(BLOCKS):
        for d in range(KEPT):
            j = (i + d) % BLOCKS
            for half in range(2):
                down = pl.ds(i * BLOCK + half * TILE, TILE)
                for column_half in range(2):
                    across = pl.ds(j * BLOCK + column_half * TILE, TILE)
                    tile = tiles[tile_rows(i, d, half, column_half), :]
                    gram[down, across] = tile
                    if d == 0:
                        own = own + square_sum(tile)
                    else:
                        others = others + square_sum(tile)
                        gram[across, down] = dot_nt(identity, tile).astype(jnp.bfloat16)
    quartic = jnp.full((1, 1), jnp.sum(own + 2.0 * others), jnp.float32)
    scale = 1.0 / jnp.sqrt(jnp.sqrt(quartic) + EPSILON)
    square = scale * scale

    state[...] = base_ref[...].astype(jnp.float32) * scale
    value[0] = state[...].astype(jnp.bfloat16)

    def step(number, _):
        now = lax.rem(number, 2)
        place = jnp.where(number < 2, number, lax.rem(number + 3, 5))
        cubic = (place == 0) | (place == 3)
        quintic = (place == 1) | (place == 4)
        keep = jnp.where(cubic, COEF_LINEAR, jnp.where(quintic, 1.0, 0.0))
        add = jnp.where(cubic, COEF_CUBIC, jnp.where(quintic, COEF_QUINTIC, 1.0))
        from_product = jnp.where(cubic, 1.0, 0.0)
        from_state = jnp.where(cubic, 0.0, 1.0)
        for strip in range(M // STRIP):
            cut = pl.ds(strip * STRIP, STRIP)
            upper = jnp.dot(
                value[now, :, : M // 2], gram[: M // 2, cut], preferred_element_type=jnp.float32
            )
            lower = jnp.dot(
                value[now, :, M // 2 :], gram[M // 2 :, cut], preferred_element_type=jnp.float32
            )
            product = square * (upper + lower)
            result = keep * state[:, cut] + add * product
            state[:, cut] = result
            value[1 - now, :, cut] = (from_product * product + from_state * result).astype(
                jnp.bfloat16
            )

        @pl.when(number == 1)
        def _():
            total[...] = COEF_LINEAR * state[...]

        @pl.when(number == 6)
        def _():
            total[...] += COEF_CUBIC * state[...]

        return 0

    lax.fori_loop(0, STEPS, step, 0)
    update = (UPDATE_SCALE * (total[...] + COEF_QUINTIC * state[...])).astype(jnp.bfloat16)
    for r in range(ROWS):
        out_ref[r] = update[:, r * OWN_ROWS : (r + 1) * OWN_ROWS]


def newton_schulz(base, parts):
    return pl.pallas_call(
        newton_schulz_kernel,
        out_shape=jax.ShapeDtypeStruct((ROWS, OWN_COLS, OWN_ROWS), jnp.bfloat16),
        in_specs=[pl.BlockSpec(memory_space=pltpu.VMEM)]
        + [pl.BlockSpec(memory_space=pl.ANY)] * len(parts),
        out_specs=pl.BlockSpec(memory_space=pltpu.VMEM),
        scratch_shapes=[
            pltpu.VMEM((GRAM_ROWS, TILE), jnp.bfloat16),
            pltpu.VMEM((M, M), jnp.bfloat16),
            pltpu.VMEM((2, OWN_COLS, M), jnp.bfloat16),
            pltpu.VMEM((OWN_COLS, M), jnp.float32),
            pltpu.VMEM((OWN_COLS, M), jnp.float32),
            pltpu.SemaphoreType.DMA((sum(len(places) for places in PARTS),)),
        ],
        compiler_params=pltpu.CompilerParams(vmem_limit_bytes=58 * 2**20),
        name="newton_schulz",
    )(base, *parts)


def add_up(parts):
    total = parts[0].astype(jnp.float32)
    for part in parts[1:]:
        total = total + part.astype(jnp.float32)
    return total.astype(jnp.bfloat16)


def scattered_sum(chunks, others):
    received = [chunks[0]] + [over_x(chunks[k], k) for k in (2, 1, 3)]
    others = over_z(others)
    others = add_up([others[z] for z in range(Z_CHIPS)]).reshape(X_CHIPS, OTHER_SHARE, TILE)
    others = [others[0]] + [over_x(others[k], k) for k in (2, 1, 3)]
    shares = over_z(add_up(received).reshape(Z_CHIPS, FIRST_SHARE, TILE))
    return jnp.concatenate([add_up([shares[z] for z in range(Z_CHIPS)]), add_up(others)])


def gathered(share):
    chunk = over_z(jnp.broadcast_to(share[None], (Z_CHIPS, SHARE, TILE)))
    chunk = [chunk[:, :FIRST_SHARE], chunk[:, FIRST_SHARE:]]
    chunk = jnp.concatenate([part.reshape(-1, TILE) for part in chunk])
    first, second = chunk[:HALF_CHUNK], chunk[HALF_CHUNK:]
    from_x = {k: over_x(first, k) for k in (1, 3, 2)}
    from_y = {k: over_y(second, k) for k in (1, 3, 2)}
    first = jnp.stack([first] + [from_x[k] for k in (1, 2, 3)])
    second = jnp.stack([second] + [from_y[k] for k in (1, 2, 3)])
    first, second = lax.optimization_barrier((first, second))
    ups, downs = [over_y(first, 1), over_x(second, 1)], [over_y(first, 3), over_x(second, 3)]
    onward = [up[:2] for up in ups], [down[2:] for down in downs]
    ups, downs, onward = lax.optimization_barrier((ups, downs, onward))
    far = []
    for over, up, down in zip((over_y, over_x), *onward):
        far += [over(up, 1), over(down, 3)]
    near = over_cores(jnp.concatenate([first, second] + ups + downs))
    sent, near = lax.optimization_barrier((far, near))
    own_core = [first, second] + ups + downs + far
    return own_core + [near, over_cores(jnp.concatenate(sent))]


def per_device(gradient, momentum):
    grad32 = gradient.astype(jnp.float32)
    buffer = MOMENTUM_DECAY * momentum + grad32
    nesterov = grad32 + MOMENTUM_DECAY * buffer
    base = nesterov.astype(jnp.bfloat16)
    shifted = {k: over_y(base, k) for k in (1, 3, 2)}
    rows = [base] + [shifted[k] for k in (1, 2, 3)]
    chunks, others, columns = partial_gram(rows + [over_cores(part) for part in rows])
    parts = gathered(scattered_sum(chunks, others))
    update = newton_schulz(columns, parts)
    update = lax.all_to_all(update, "row", split_axis=0, concat_axis=0)
    update_matrix = update.reshape(PANEL_COLS, OWN_ROWS).T
    gradient, momentum = lax.optimization_barrier((gradient, momentum))
    buffer = MOMENTUM_DECAY * momentum + gradient.astype(jnp.float32)
    return (update_matrix, buffer)


def solution(mesh):
    return jax.shard_map(
        per_device,
        mesh=mesh,
        in_specs=(P("row", "col"), P("row", "col")),
        out_specs=(P("row", "col"), P("row", "col")),
        check_vma=False,
    )
```
